512 devices in a mesh: tmpl: 32 (over x, y_hi, core), stn: 16 (over y_lo, z).
Axes of the slice: x: 4, y: 8 (y_hi: 4, y_lo: 2; y = y_hi * 2 + y_lo), z: 8, core: 2. Of those that a mesh axis runs over, the one named last changes fastest.
Arguments:
- data: bfloat16 [2, 96, 3, 1024], P(None, 'stn', None, 'tmpl'), may hold values from -6 to 6
- waves: bfloat16 [96, 512, 3, 300], P('stn', 'tmpl'), may hold values from -6 to 6
- slot_group: int32 [96, 512, 1], P('stn', 'tmpl'), may hold values from 0 to 31; in each aligned block of 16 rows (0 to 15, 16 to 31, ..., all dimensions but the last counted through in order) at most 2 rows name the same one
- slot_local: int32 [96, 512], P('stn', 'tmpl'), may hold values from 0 to 255
- moveout: int32 [96, 512], P('stn', 'tmpl'), may hold values from 0 to 469
- chan_mask: int32 [96, 3], P('stn'), may hold values 0 or 1
Outputs:
- scores: float32 [2, 8192, 256], P(None, ('tmpl', 'stn'))
The draws below stay inside these ranges and needn't reach their ends.
Inputs may be any that keep to these rules, and one draw needn't show every extreme that they name: `slot_group`: among the 16 slots k*16 to (k+1)*16 - 1 of one station, no template group is named more than 2 times.
All inputs are finite; a program needn't handle non-finite values. No bound on the sum of `chan_mask` on one device may be relied on, other than what follows from the above.
Results may differ from the reference program's by a relative error of at most 0.0029.
Values may be sent and summed in bfloat16 or wider, within the bound.
A program may use at most 128 MiB of HBM per device.

```python
import math
import jax
import jax.numpy as jnp
import numpy as np
from jax import lax

TAPS = 300
COMP = 3
W = 1024
NK = 256
BLOCKS = 2
SLOT_DEV = 16
TPD = 16
MAXSHIFT = 469
MOST = 2
TG = 256
TEMPLATES = 8192
STATIONS = 96
SLOTS = 512
N_TMPL = 32
N_STN = 16


def plant(drawn, key, smallest, largest):
    dims = drawn.shape
    spot = [jax.random.randint(jax.random.fold_in(key, axis), (), 0, dims[axis]) for axis in range(len(dims))]
    drawn = drawn.at[tuple(spot)].set(smallest)
    longest = dims.index(max(dims))
    spot[longest] = (spot[longest] + 1) % dims[longest]
    return drawn.at[tuple(spot)].set(largest)


def block_levels(own_key, extent, split, least, high):
    level, own = 1.0, jax.random.fold_in(own_key, 6)
    for position, shards_of in split:
        steps = jnp.exp(jax.random.uniform(jax.random.fold_in(own, position), (shards_of,), jnp.float32, least / len(split), high / len(split)))
        level = level * jnp.repeat(steps, extent[position] // shards_of).reshape([-1 if axis == position else 1 for axis in range(len(extent))])
    return level


def cumulative_ranks(amount, skew):
    portions = [(1 << 20) // math.isqrt(standing ** skew) + 1 for standing in range(1, amount + 1)]
    scale = 1 + sum(portions) // (1 << 30)
    return np.cumsum(np.array([max(1, weight // scale) for weight in portions]))


def skewed_ids(own_key, extent, number_of, slope):
    table = cumulative_ranks(number_of, slope)
    pick = jax.random.randint(jax.random.fold_in(own_key, 1), extent, 0, int(table[number_of - 1]))
    rank = jnp.searchsorted(jnp.asarray(table, jnp.int32), pick, side="right")
    return jax.random.permutation(jax.random.fold_in(own_key, 2), number_of)[rank].astype(jnp.int32)


def assign_block(stream_key, own, number, rows, amount, top, most, slope):
    sequence = jax.random.permutation(stream_key, amount)
    packed, ordinary = portions_of(amount, rows * top, most, slope, True), portions_of(amount, rows * top, most, slope, False)
    places = jnp.arange(amount)

    def named(sizes, offset_by):
        used = int((sizes > 0).sum())
        fixed = max(1, used // 4)
        passed = fixed + (places - fixed + offset_by * (used - fixed)) % max(1, amount - fixed)
        return jnp.zeros((amount,), jnp.int32).at[sequence[jnp.where(places < fixed, places, passed)]].set(jnp.asarray(sizes, jnp.int32))

    sizes = jnp.where(number % 4 == 0, named(packed, number // 4), named(ordinary, number - number // 4 - 1))
    mixed = jax.random.permutation(jax.random.fold_in(own, 3), amount)
    donor, sink = mixed[0:amount // 2 * 2:2], mixed[1:amount // 2 * 2:2]
    room = jnp.minimum(sizes[donor] - 1, most - sizes[sink]) // 2
    room = jnp.where((donor == sequence[0]) | (sink == sequence[0]) | (sizes[sink] == 0), 0, jnp.maximum(room, 0))
    passed = jax.random.randint(jax.random.fold_in(own, 4), (amount // 2,), 0, 1 << 20) % (room + 1)
    sizes = sizes.at[donor].add(-passed).at[sink].add(passed)
    items = jnp.searchsorted(jnp.cumsum(sizes), jnp.arange(rows * top), side="right").astype(jnp.int32)
    table = items.reshape(top, rows).T
    table = table[jax.random.permutation(jax.random.fold_in(own, 1), rows)]
    offset_by = jax.random.randint(jax.random.fold_in(own, 2), (rows, 1), 0, top)
    return jnp.take_along_axis(table, (jnp.arange(top)[None, :] + offset_by) % top, axis=1)


def portions_of(number_of, total, bound, slope, full):
    portions = [(1 << 20) // math.isqrt(rank ** slope) + 1 for rank in range(1, number_of + 1)]
    largest = bound if full else min(bound, max(-(-total // number_of), total * portions[0] // sum(portions)))
    least = 1 if total - largest >= number_of - 1 else 0
    given, rest = [largest] + [least] * (number_of - 1), total - largest - least * (number_of - 1)
    while rest > 0:
        free = [i for i in range(1, number_of) if given[i] < largest] or [i for i in range(1, number_of) if given[i] < bound]
        whole, left = sum([portions[i] for i in free]), rest
        for i in free:
            extra = min(bound - given[i], max(1, left * portions[i] // whole), rest)
            given[i] = given[i] + extra
            rest = rest - extra
    return np.array(given)


def noise(key, shape, deviation, limit, shards=(), held_as=jnp.bfloat16):
    entries = jax.random.normal(key, shape, jnp.float32) * deviation
    if len(shards) > 0:
        entries = block_levels(key, shape, shards, -0.22, 0.18) * entries
    return jnp.clip(entries, min=-limit, max=limit).astype(held_as)


def setup_inputs(seed: int = 0) -> dict:
    splits = jax.random.split(jax.random.key(seed), 7)
    data = noise(splits[0], (BLOCKS, STATIONS, COMP, W), 1.0, 6.0, ((1, 16), (3, 32)))
    waves = noise(splits[1], (STATIONS, SLOTS, COMP, TAPS), 1.0, 6.0, ((0, 16), (1, 32)))
    slot_group_keys = jax.random.split(jax.random.fold_in(splits[2], 1), STATIONS * SLOTS // SLOT_DEV)
    slot_group_turns = jax.random.permutation(jax.random.fold_in(splits[2], 3), STATIONS * SLOTS // SLOT_DEV)
    slot_group = jax.vmap(lambda own, number: assign_block(jax.random.fold_in(splits[2], 2), own, number, SLOT_DEV, N_TMPL, 1, MOST, 2))(slot_group_keys, slot_group_turns).reshape((STATIONS, SLOTS, 1))
    slot_local = plant(skewed_ids(splits[3], (STATIONS, SLOTS), TG, 2), jax.random.fold_in(splits[3], 3), 0, TG - 1).astype(jnp.int32)
    moveout = plant(jax.random.randint(splits[4], (STATIONS, SLOTS), 0, MAXSHIFT + 1), jax.random.fold_in(splits[4], 1), 0, MAXSHIFT).astype(jnp.int32)
    chan_mask = plant((jax.random.randint(splits[5], (STATIONS, COMP), 0, 4) < 3).astype(jnp.int32), jax.random.fold_in(splits[5], 1), 0, 1)
    return {"data": data, "waves": waves, "slot_group": slot_group, "slot_local": slot_local, "moveout": moveout, "chan_mask": chan_mask}


epsilon = 1e-06

def window_rows(series, tap_count, lag_count):
    index_grid = jnp.arange(tap_count)[:, None] + jnp.arange(lag_count)[None, :]
    return series[..., index_grid]

def reference(data, waves, slot_group, slot_local, moveout, chan_mask):
    per_group = TPD * N_STN
    lag_count = W - TAPS + 1

    def station_step(running, inputs):
        stack_sums, counts = running
        station_data, station_waves, group_ids, local_ids, shift_by, station_mask = inputs
        hankel_rows = window_rows(station_data.astype(jnp.float32), TAPS, lag_count)
        data_power = lax.optimization_barrier(jnp.sum(hankel_rows * hankel_rows, axis=2)) / TAPS
        wave_float = station_waves.astype(jnp.float32)
        wave_power = lax.optimization_barrier(jnp.sum(wave_float * wave_float, axis=2)) / TAPS
        numerator = jnp.einsum('pcj,bcjk->pbck', wave_float, hankel_rows)
        denominator = TAPS * jnp.sqrt(wave_power + epsilon)[:, None, :, None] * jnp.sqrt(data_power + epsilon)[None]
        mask_float = station_mask.astype(jnp.float32)
        channel_sum = lax.optimization_barrier(jnp.sum(numerator / denominator * mask_float[None, None, :, None], axis=2))
        correlation = (channel_sum / jnp.maximum(jnp.sum(mask_float), 1.0)).astype(jnp.bfloat16)
        lag_index = shift_by[:, None, None] + jnp.arange(NK)[None, None, :]
        lag_index = jnp.broadcast_to(lag_index, (SLOTS, BLOCKS, NK))
        shifted = jnp.take_along_axis(correlation, lag_index, axis=2).astype(jnp.float32)
        template_ids = group_ids[:, 0] * per_group + local_ids
        stack_sums = stack_sums.at[template_ids].add(shifted)
        counts = counts.at[template_ids].add(jnp.ones((SLOTS,), jnp.float32))
        return ((stack_sums, counts), None)
    initial = (jnp.zeros((TEMPLATES, BLOCKS, NK), jnp.float32), jnp.zeros((TEMPLATES,), jnp.float32))
    (stack_sums, counts), ignored = lax.scan(station_step, initial, (jnp.moveaxis(data, 1, 0), waves, slot_group, slot_local, moveout, chan_mask))
    scores = jnp.sqrt(jnp.float32(TAPS)) * stack_sums / jnp.sqrt(jnp.maximum(counts, 1.0))[:, None, None]
    return jnp.moveaxis(scores, 0, 1)
```

```python
import functools

import jax
import jax.numpy as jnp
from jax import lax
from jax.experimental import pallas as pl
from jax.experimental.pallas import tpu as pltpu
from jax.sharding import PartitionSpec as P

NT = 32
NS = 16
TAPS = 300
EPS = 1e-06
MESH = pl.DeviceIdType.MESH
f32, bf16, i32 = jnp.float32, jnp.bfloat16, jnp.int32


def iota(shape, axis):
    return lax.broadcasted_iota(i32, shape, axis)


def left(x, by):
    by %= 128
    return x if by == 0 else pltpu.roll(x, 128 - by, axis=x.ndim - 1)


def next_block(x):
    half = (iota(x.shape, x.ndim - 1) >> 5) & 1
    return jnp.where(half == 0, left(x, 32), left(x, -31))


def split2(x):
    hi = x.astype(bf16)
    return hi, (x - hi.astype(f32)).astype(bf16)


def dot(a, b):
    return jnp.dot(a, b, preferred_element_type=f32)


def kernel(
    cm, dtile, w0, pk, gl, out,
    send_a, recv_a, wt, invw, tsel, pb, vb, z0, zf, ssc,
    send_b, recv_b, key, ob, acc, send_c, recv_c, send_k, recv_k, q,
    sa, ra, sb, rb, sc_, rc, sk, rk,
):
    me_t, me_n = lax.axis_index("tmpl"), lax.axis_index("stn")

    bar = pltpu.get_barrier_semaphore()

    def greet_t(j, _):
        pl.semaphore_signal(bar, inc=1, device_id={"tmpl": lax.rem(me_t + j, NT)}, device_id_type=MESH)
        return 0

    def greet_n(j, _):
        pl.semaphore_signal(bar, inc=1, device_id={"stn": lax.rem(me_n + j, NS)}, device_id_type=MESH)
        return 0

    lax.fori_loop(1, NT, greet_t, 0)
    lax.fori_loop(1, NS, greet_n, 0)

    lane = iota((96, 128), 1)
    packed = pk[...]
    mine = (lane >> 4) == lax.rem(me_t, 8)
    id_rows = jnp.where(mine & (((lane >> 2) & 3) == (packed & 3)), (packed >> 2) & 511, 0)
    pick = iota((512, 96), 0) == gl[3:4, 0:96]
    ids = dot(pick.astype(f32).astype(bf16), id_rows.astype(f32).astype(bf16))
    send_a[...] = (ids.reshape(NT, 16, 128) + dtile[...].astype(f32)[None]).astype(bf16)
    recv_a[me_t] = send_a[me_t]

    pl.semaphore_wait(bar, NT - 1 + NS - 1)

    def send_first(j, _):
        peer = lax.rem(me_t + j, NT)
        pltpu.make_async_remote_copy(
            src_ref=send_a.at[peer], dst_ref=recv_a.at[me_t], send_sem=sa, recv_sem=ra,
            device_id={"tmpl": peer}, device_id_type=MESH).start()
        return 0

    lax.fori_loop(1, NT, send_first, 0)

    def prepare(s, _):
        rows = pk[pl.ds(pl.multiple_of(s * 16, 16), 16), :]
        fine = (rows >> 11) & 31
        lane16 = iota((16, 128), 1)
        usable = [cm[s, c].astype(f32) for c in range(3)]
        total = usable[0] + usable[1] + usable[2]
        per = jnp.where(total > 2.5, 1.0 / 3.0, jnp.where(total > 1.5, 0.5, 1.0)) / TAPS
        for c in range(3):
            sc = s * 3 + c
            x = [w0[sc, :, 128 * j:128 * j + 128].astype(f32) for j in range(3)]
            power = jnp.sum(x[0] * x[0] + x[1] * x[1] + x[2] * x[2], axis=1, keepdims=True)
            invw[sc] = jnp.broadcast_to(lax.rsqrt(power / TAPS + EPS), (16, 128)) * (usable[c] * per)
            for bit in range(5):
                by = 1 << bit
                y = [pltpu.roll(v, by, axis=1) for v in x]
                wide = [jnp.where(lane16 >= by, y[j], y[j - 1] if j else 0.0) for j in range(3)]
                on = (fine & by) != 0
                x = [jnp.where(on, wide[j], x[j]) for j in range(3)]
            k0 = iota((16, 16, 128), 1)
            l3 = iota((16, 16, 128), 2)
            y = [
                pltpu.roll(jnp.broadcast_to(v[:, None, :], (16, 16, 128)), 0, axis=2, stride=1, stride_axis=1)
                for v in x
            ]
            for j in range(3):
                t = jnp.where(l3 >= k0, y[j], y[j - 1] if j else 0.0)
                wt[sc, :, 128 * j:128 * j + 128] = t.reshape(256, 128).astype(bf16)
        k0 = iota((16, 16, 128), 1)
        l3 = iota((16, 16, 128), 2)
        hit = (l3 & 63) == k0 + fine[:, None, :]
        tsel[s] = jnp.where(hit, 1.0, 0.0).reshape(256, 128).astype(bf16)
        return 0

    lax.fori_loop(0, 6, prepare, 0)

    for r in range(3):
        pb[r] = jnp.where(iota((512, 128), 0) == gl[r:r + 1, :], 1.0, 0.0).astype(bf16)

    pltpu.make_async_copy(send_a.at[pl.ds(0, NT - 1)], recv_a.at[pl.ds(0, NT - 1)], ra).wait()
    zf[...] = recv_a[...].astype(f32).reshape(512, 128)
    for g in range(3):
        rows = [zf[pl.ds(4 * g + bh, NT, stride=16), :] for bh in range(4)]
        z0[128 * g:128 * g + 128, :] = jnp.concatenate(rows, axis=0).T

    row = iota((512, 256), 0)
    col = iota((512, 256), 1)
    same = ((row >> 4) & 7) == ((col >> 4) & 7)
    k0, r, kind = row & 15, col & 15, row >> 7
    inside = jnp.where(
        kind == 0, (r >= k0).astype(i32),
        jnp.where(kind == 1, 1, jnp.where(kind == 2, (r < k0 + 12).astype(i32), (r < k0 - 4).astype(i32))))
    windows = jnp.where(same, inside, 0).astype(f32).astype(bf16)
    for g in range(3):
        z = z0[128 * g:128 * g + 128, :]
        hi, lo = split2(z * z)
        sums = dot(windows, jnp.concatenate([hi, lo], axis=0))
        suffix, whole, e1, e2 = (sums[128 * i:128 * i + 128] for i in range(4))
        b2 = whole + next_block(whole)
        b4 = b2 + left(b2, 1)
        b8 = b4 + left(b4, 2)
        b16 = b8 + left(b8, 4)
        power = suffix + left(e1, 9) + next_block(b16 + left(whole, 8) + left(e2, 9))
        v = lax.rsqrt(power / TAPS + EPS)
        parts = [split2(x) for x in (v, next_block(v), left(v, 1))]
        for k in range(8):
            sc = 8 * g + k
            if sc >= 18:
                break
            for e in range(3):
                for part in range(2):
                    vb[sc // 3, 64 * part + 16 * e:64 * part + 16 * e + 16, 128 * (sc % 3):128 * (sc % 3) + 128] = (
                        parts[e][part][16 * k:16 * k + 16])
            for part in range(2):
                vb[sc // 3, 64 * part + 48:64 * part + 64, 128 * (sc % 3):128 * (sc % 3) + 128] = (
                    jnp.zeros((16, 128), bf16))

    def pair(rr, _):
        lane16 = iota((16, 128), 1)
        pieces = [[None, None] for _ in range(4)]
        for s2 in range(2):
            s = rr * 2 + s2
            norm = dot(tsel[s], vb[s])
            total = None
            for c in range(3):
                sc = s * 3 + c
                z = z0[pl.ds(pl.multiple_of(sc * 16, 16), 16), :]
                z1 = next_block(z)
                lagged = jnp.concatenate(
                    [left(x, u) for u in range(12) for x in (z, z1)], axis=0).astype(bf16)
                numer = dot(wt[sc], lagged)
                scaled = norm[:, 128 * c:128 * c + 128].reshape(16, 16, 128) * invw[sc][:, None, :]
                term = numer.reshape(16, 16, 128) * scaled
                total = term if total is None else total + term
            ssc[s2] = total.reshape(256, 128)
            coarse = pk[pl.ds(pl.multiple_of(s * 16, 16), 16), :] >> 16
            for chunk in range(4):
                merged = None
                for low in range(4):
                    x = ssc[s2, pl.ds(4 * chunk + low, 16, stride=16), :]
                    for bit in range(4):
                        x = jnp.where((coarse & (1 << bit)) != 0, left(x, 1 << bit), x)
                    x = left(x, -8 * low)
                    merged = x if merged is None else jnp.where(((lane16 >> 3) & 3) == low, x, merged)
                pieces[chunk][s2] = merged
        corr = jnp.concatenate([x for two in pieces for x in two], axis=0).astype(bf16)
        send_b[rr] = dot(pb[rr], corr).astype(bf16).reshape(NT, 16, 128)
        recv_b[rr, me_t] = send_b[rr, me_t]

        def send_second(j, _):
            peer = lax.rem(me_t + j, NT)
            pltpu.make_async_remote_copy(
                src_ref=send_b.at[rr, peer], dst_ref=recv_b.at[rr, me_t], send_sem=sb.at[rr], recv_sem=rb.at[rr],
                device_id={"tmpl": peer}, device_id_type=MESH).start()
            return 0

        lax.fori_loop(1, NT, send_second, 0)
        return 0

    lax.fori_loop(0, 3, pair, 0)

    lane32 = iota((1, 128), 1)
    for rr in range(3):
        marks = zf[pl.ds(12 + rr, NT, stride=16), :]
        for u in range(4):
            mark = jnp.sum(marks[8 * u:8 * u + 8], axis=0, keepdims=True).astype(i32)
            key[4 * rr + u:4 * rr + u + 1, :] = jnp.where(mark > 0, (lane32 & 3) * 256 + mark - 1, -1)

    def onehot(n, _):
        line = iota((64, 128), 0)
        code = ((line >> 4) & 3) * 256 + (line & 15) + n * 16
        found = None
        start = pl.multiple_of(n * 64, 64)
        for rr in range(3):
            for u in range(4):
                hit = jnp.where(code == key[4 * rr + u:4 * rr + u + 1, :], 1.0, 0.0)
                ob[rr, pl.ds(start, 64), 128 * u:128 * u + 128] = hit.astype(bf16)
                found = hit[:16] if found is None else found + hit[:16]
        number = jnp.broadcast_to(jnp.sum(found, axis=1, keepdims=True), (16, 128)).astype(i32)
        parts = jnp.where(iota((16, 128), 1) < 64, number & 127, number >> 7)
        send_k[n] = parts.astype(f32).astype(bf16)
        return 0

    lax.fori_loop(0, NS, onehot, 0)
    recv_k[me_n] = send_k[me_n]

    def send_counts(j, _):
        peer = lax.rem(me_n + j, NS)
        pltpu.make_async_remote_copy(
            src_ref=send_k.at[peer], dst_ref=recv_k.at[me_n], send_sem=sk, recv_sem=rk,
            device_id={"stn": peer}, device_id_type=MESH).start()
        return 0

    lax.fori_loop(1, NS, send_counts, 0)

    k = iota((512, 512), 1)
    place = ((k >> 2) & 3) * 128 + (k >> 8) * 64 + ((k >> 4) & 1) * 32 + (k & 3) * 8 + ((k >> 5) & 7)
    q[...] = jnp.where(iota((512, 512), 0) == place, 1.0, 0.0).astype(bf16)

    for rr in range(2):
        pltpu.make_async_copy(send_b.at[rr, pl.ds(0, NT - 1)], recv_b.at[rr, pl.ds(0, NT - 1)], rb.at[rr]).wait()
        part = dot(ob[rr], recv_b[rr].reshape(512, 128))
        if rr == 0:
            acc[...] = part
        else:
            acc[...] += part
    pltpu.make_async_copy(send_b.at[2, pl.ds(0, NT - 1)], recv_b.at[2, pl.ds(0, NT - 1)], rb.at[2]).wait()
    part = acc[...] + dot(ob[2], recv_b[2].reshape(512, 128))
    send_c[...] = part.astype(bf16).reshape(NS, 64, 128)
    recv_c[me_n] = send_c[me_n]

    def send_stacks(j, _):
        peer = lax.rem(me_n + j, NS)
        pltpu.make_async_remote_copy(
            src_ref=send_c.at[peer], dst_ref=recv_c.at[me_n], send_sem=sc_, recv_sem=rc,
            device_id={"stn": peer}, device_id_type=MESH).start()
        return 0

    lax.fori_loop(1, NS, send_stacks, 0)

    pltpu.make_async_copy(send_k.at[pl.ds(0, NS - 1)], recv_k.at[pl.ds(0, NS - 1)], rk).wait()
    found = jnp.sum(recv_k[...].astype(f32), axis=0)
    found = jnp.where(iota((16, 128), 1) < 64, found, found * 128.0)
    found = found + left(found, 64)
    scale = jnp.sqrt(f32(TAPS)) * lax.rsqrt(jnp.maximum(found, 1.0))

    pltpu.make_async_copy(send_c.at[pl.ds(0, NS - 1)], recv_c.at[pl.ds(0, NS - 1)], rc).wait()
    y = jnp.sum(recv_c[...].astype(f32), axis=0).reshape(4, 16, 128) * scale[None]
    y = jnp.concatenate([y[0], y[1], y[2], y[3]], axis=1)
    hi, rest = y.astype(bf16), y - y.astype(bf16).astype(f32)
    mid, low = split2(rest)
    moved = dot(jnp.concatenate([hi, mid, low], axis=0), q[...])
    moved = moved[0:16] + moved[16:32] + moved[32:48]
    out[0] = moved[:, :256]
    out[1] = moved[:, 256:]

    pltpu.make_async_copy(send_a.at[pl.ds(0, NT - 1)], recv_a.at[pl.ds(0, NT - 1)], sa).wait()
    for rr in range(3):
        pltpu.make_async_copy(send_b.at[rr, pl.ds(0, NT - 1)], recv_b.at[rr, pl.ds(0, NT - 1)], sb.at[rr]).wait()
    pltpu.make_async_copy(send_k.at[pl.ds(0, NS - 1)], recv_k.at[pl.ds(0, NS - 1)], sk).wait()
    pltpu.make_async_copy(send_c.at[pl.ds(0, NS - 1)], recv_c.at[pl.ds(0, NS - 1)], sc_).wait()


def body(data, waves, slot_group, slot_local, moveout, chan_mask):
    d = jnp.pad(data.reshape(2, 18, 2, 16), ((0, 0), (0, 6), (0, 0), (0, 0)))
    d = d.reshape(2, 3, 8, 2, 16).transpose(1, 0, 3, 2, 4).reshape(12, 128)
    dtile = jnp.pad(d, ((0, 4), (0, 0)))
    w0 = jnp.pad(jnp.transpose(waves, (0, 2, 1, 3)).reshape(18, 16, TAPS), ((0, 0), (0, 0), (0, 384 - TAPS)))
    group = slot_group[..., 0]
    earlier = jnp.arange(16)[None, :] < jnp.arange(16)[:, None]
    rank = jnp.sum(((group[:, :, None] == group[:, None, :]) & earlier[None]).astype(i32), axis=2)
    station = jnp.arange(6, dtype=i32)[:, None]
    quarter = (station & 1) * 2 + rank
    pk = (moveout << 11) | ((slot_local + 1) << 2) | quarter
    pk = jnp.broadcast_to(pk.reshape(96, 1), (96, 128))
    where = (group * 16 + quarter * 4).reshape(3, 1, 32)
    where = (where + jnp.arange(4, dtype=i32)[None, :, None]).reshape(3, 128)
    first = (group * 16 + 12 + (station >> 1)).reshape(1, 96)
    gl = jnp.concatenate([where, jnp.pad(first, ((0, 0), (0, 32)), constant_values=-1)], axis=0)
    gl = jnp.pad(gl, ((0, 4), (0, 0)))
    vmem = pl.BlockSpec(memory_space=pltpu.VMEM)
    dma = pltpu.SemaphoreType.DMA
    return pl.pallas_call(
        kernel,
        out_shape=jax.ShapeDtypeStruct((2, 16, 256), f32),
        in_specs=[pl.BlockSpec(memory_space=pltpu.SMEM), vmem, vmem, vmem, vmem],
        out_specs=vmem,
        scratch_shapes=[
            pltpu.VMEM((NT, 16, 128), bf16),
            pltpu.VMEM((NT, 16, 128), bf16),
            pltpu.VMEM((18, 256, 384), bf16),
            pltpu.VMEM((18, 16, 128), f32),
            pltpu.VMEM((6, 256, 128), bf16),
            pltpu.VMEM((3, 512, 128), bf16),
            pltpu.VMEM((6, 128, 384), bf16),
            pltpu.VMEM((384, 128), f32),
            pltpu.VMEM((512, 128), f32),
            pltpu.VMEM((2, 256, 128), f32),
            pltpu.VMEM((3, NT, 16, 128), bf16),
            pltpu.VMEM((3, NT, 16, 128), bf16),
            pltpu.VMEM((16, 128), i32),
            pltpu.VMEM((3, 1024, 512), bf16),
            pltpu.VMEM((1024, 128), f32),
            pltpu.VMEM((NS, 64, 128), bf16),
            pltpu.VMEM((NS, 64, 128), bf16),
            pltpu.VMEM((NS, 16, 128), bf16),
            pltpu.VMEM((NS, 16, 128), bf16),
            pltpu.VMEM((512, 512), bf16),
            dma, dma, dma((3,)), dma((3,)), dma, dma, dma, dma,
        ],
        compiler_params=pltpu.CompilerParams(
            collective_id=0, has_side_effects=True, vmem_limit_bytes=48 * 2**20),
    )(chan_mask, dtile, w0, pk, gl)


def solution(mesh):
    in_specs = (
        P(None, "stn", None, "tmpl"),
        P("stn", "tmpl", None, None),
        P("stn", "tmpl", None),
        P("stn", "tmpl"),
        P("stn", "tmpl"),
        P("stn", None),
    )
    out_specs = P(None, ("tmpl", "stn"), None)
    return jax.shard_map(body, mesh=mesh, in_specs=in_specs, out_specs=out_specs, check_vma=False)
```

```python
import functools

import jax
import jax.numpy as jnp
from jax import lax
from jax.experimental import pallas as pl
from jax.experimental.pallas import tpu as pltpu
from jax.sharding import PartitionSpec as P

NT = 32
NS = 16
TAPS = 300
EPS = 1e-06
MESH = pl.DeviceIdType.MESH
f32, bf16, i32 = jnp.float32, jnp.bfloat16, jnp.int32


def iota(shape, axis):
    return lax.broadcasted_iota(i32, shape, axis)


def left(x, by):
    by %= 128
    return x if by == 0 else pltpu.roll(x, 128 - by, axis=x.ndim - 1)


def next_block(x):
    half = (iota(x.shape, x.ndim - 1) >> 5) & 1
    return jnp.where(half == 0, left(x, 32), left(x, -31))


def split2(x):
    hi = x.astype(bf16)
    return hi, (x - hi.astype(f32)).astype(bf16)


def dot(a, b):
    return jnp.dot(a, b, preferred_element_type=f32)


def far_first(j):
    return jnp.where(j < 2, 2 - j, 9 - 3 * j)


def tmpl_peer(me, j):
    y = far_first(j >> 3)
    x = far_first((j >> 1) & 3)
    return ((((me >> 3) + x) & 3) << 3) | ((((me >> 1) + y) & 3) << 1) | ((me + 1 + j) & 1)


def stn_peer(me, j):
    a = j >> 1
    z = jnp.where((a & 1) == 1, 4 - ((a + 1) >> 1), 4 + (a >> 1))
    return ((((me >> 3) + 1 + j) & 1) << 3) | ((me + z) & 7)


def kernel(
    data_in, waves_in, group_in, local_in, move_in, mask_in, out,
    data_v, w0, group_v, local_v, move_v, cm, pk, codes,
    send_a, recv_a, wt, invw, tsel, pb, windows, z0, zf, ssc,
    send_b, recv_b, key, ob, acc, send_c, recv_c, send_k, recv_k, q,
    si, sw, sa, ra, sb, rb, sc_, rc, sk, rk,
):
    me_t, me_n = lax.axis_index("tmpl"), lax.axis_index("stn")
    small = [
        pltpu.make_async_copy(data_in, data_v.at[pl.ds(0, 18)], si.at[0]),
        pltpu.make_async_copy(group_in, group_v, si.at[1]),
        pltpu.make_async_copy(local_in, local_v, si.at[2]),
        pltpu.make_async_copy(move_in, move_v, si.at[3]),
        pltpu.make_async_copy(mask_in, cm, si.at[4]),
    ]
    large = pltpu.make_async_copy(waves_in, w0, sw)
    for copy in small:
        copy.start()
    large.start()

    bar = pltpu.get_barrier_semaphore()

    def greet_t(j, _):
        pl.semaphore_signal(bar, inc=1, device_id={"tmpl": tmpl_peer(me_t, j)}, device_id_type=MESH)
        return 0

    def greet_n(j, _):
        pl.semaphore_signal(bar, inc=1, device_id={"stn": stn_peer(me_n, j)}, device_id_type=MESH)
        return 0

    lax.fori_loop(0, NT - 1, greet_t, 0)
    lax.fori_loop(0, NS - 1, greet_n, 0)
    for copy in small:
        copy.wait()

    sub16, lane16s = iota((16, 16), 0), iota((16, 16), 1)
    codes[...] = jnp.zeros((8, 128), i32)
    for s in range(6):
        group = jnp.broadcast_to(group_v[s], (16, 16))
        column = jnp.sum(jnp.where(sub16 == lane16s, group, 0).astype(f32), axis=1, keepdims=True).astype(i32)
        same = group == column
        rank_rows = jnp.sum(jnp.where(same & (lane16s < sub16), 1.0, 0.0), axis=1, keepdims=True)
        rank_lanes = jnp.sum(jnp.where(same & (sub16 < lane16s), 1.0, 0.0), axis=0, keepdims=True)
        fields = (move_v[s:s + 1, :] << 11) | ((local_v[s:s + 1, :] + 1) << 2) | ((s & 1) * 2)
        fields = jnp.where(sub16 == lane16s, jnp.broadcast_to(fields, (16, 16)), 0)
        fields = jnp.sum(fields.astype(f32), axis=1, keepdims=True) + rank_rows
        pk[16 * s:16 * s + 16, :] = jnp.broadcast_to(fields, (16, 128)).astype(i32)
        codes[s:s + 1, 0:16] = group_v[s] * 16 + ((s & 1) * 2 + rank_lanes.astype(i32)) * 4
    spread = pltpu.roll(codes[...].astype(f32), 0, axis=1, stride=16, stride_axis=0)
    code = jnp.sum(spread, axis=0, keepdims=True).astype(i32)

    parts = []
    row24, lane24 = iota((24, 128), 0), iota((24, 128), 1)
    third = (row24 >= 6).astype(i32) + (row24 >= 12).astype(i32)
    keep = ((lane24 >> 4) == row24 - 6 * third) & (row24 < 18)
    for b in range(2):
        samples = data_v[:, b, :]
        for half in range(2):
            widen = iota((32, 128), 0) == half * 16 + (iota((32, 128), 1) & 15)
            parts.append(jnp.where(keep, dot(samples, jnp.where(widen, 1.0, 0.0).astype(bf16)), 0.0))
    source = iota((16, 128), 1)
    dest = iota((16, 128), 0)
    bh = (source >= 24).astype(i32) + (source >= 48).astype(i32) + (source >= 72).astype(i32)
    sc24 = source - 24 * bh
    gather = dest == ((sc24 >= 6).astype(i32) + (sc24 >= 12).astype(i32)) * 4 + bh
    gather = jnp.where(gather & (sc24 < 18) & (source < 96), 1.0, 0.0).astype(bf16)
    stacked = jnp.concatenate(parts + [jnp.zeros((32, 128), f32)], axis=0).astype(bf16)
    dtile = dot(gather, stacked)
    lane = iota((96, 128), 1)
    packed = pk[...]
    mine = (lane >> 4) == (me_t & 7)
    id_rows = jnp.where(mine & (((lane >> 2) & 3) == (packed & 3)), (packed >> 2) & 511, 0)
    first = (code & -16) + 12 + (iota((1, 128), 1) >> 5)
    pick = iota((512, 96), 0) == first[:, 0:96]
    ids = dot(jnp.where(pick, 1.0, 0.0).astype(bf16), id_rows.astype(f32).astype(bf16))
    send_a[...] = (ids.reshape(NT, 16, 128) + dtile[None]).astype(bf16)
    recv_a[me_t] = send_a[me_t]

    pl.semaphore_wait(bar, NT - 1 + NS - 1)

    def send_first(j, _):
        peer = tmpl_peer(me_t, j)
        pltpu.make_async_remote_copy(
            src_ref=send_a.at[peer], dst_ref=recv_a.at[me_t], send_sem=sa, recv_sem=ra,
            device_id={"tmpl": peer}, device_id_type=MESH).start()
        return 0

    lax.fori_loop(0, NT - 1, send_first, 0)

    large.wait()

    def prepare(s, _):
        rows = pk[pl.ds(pl.multiple_of(s * 16, 16), 16), :]
        fine = (rows >> 11) & 31
        lane16 = iota((16, 128), 1)
        usable = [cm[c, s].astype(f32) for c in range(3)]
        total = usable[0] + usable[1] + usable[2]
        per = jnp.where(total > 2.5, 1.0 / 3.0, jnp.where(total > 1.5, 0.5, 1.0)) / TAPS
        for c in range(3):
            sc = s * 3 + c
            x = [w0[sc, :, 0:128].astype(f32), w0[sc, :, 128:256].astype(f32),
                 jnp.pad(w0[sc, :, 256:TAPS].astype(f32), ((0, 0), (0, 384 - TAPS)))]
            power = jnp.sum(x[0] * x[0] + x[1] * x[1] + x[2] * x[2], axis=1, keepdims=True)
            invw[sc] = jnp.broadcast_to(lax.rsqrt(power / TAPS + EPS), (16, 128)) * (usable[c] * per)
            for bit in range(5):
                by = 1 << bit
                y = [pltpu.roll(v, by, axis=1) for v in x]
                wide = [jnp.where(lane16 >= by, y[j], y[j - 1] if j else 0.0) for j in range(3)]
                on = (fine & by) != 0
                x = [jnp.where(on, wide[j], x[j]) for j in range(3)]
            k0 = iota((16, 16, 128), 1)
            l3 = iota((16, 16, 128), 2)
            y = [
                pltpu.roll(jnp.broadcast_to(v[:, None, :], (16, 16, 128)), 0, axis=2, stride=1, stride_axis=1)
                for v in x
            ]
            for j in range(3):
                t = jnp.where(l3 >= k0, y[j], y[j - 1] if j else 0.0)
                wt[sc, :, 128 * j:128 * j + 128] = t.reshape(256, 128).astype(bf16)
        k0 = iota((16, 16, 128), 1)
        l3 = iota((16, 16, 128), 2)
        hit = (l3 & 63) == k0 + fine[:, None, :]
        tsel[s] = jnp.where(hit, 1.0, 0.0).reshape(256, 128).astype(bf16)
        return 0

    lax.fori_loop(0, 6, prepare, 0)

    chunk_of = iota((1, 128), 1) >> 5
    for r in range(3):
        placed = jnp.where(chunk_of == 0, left(code, 32 * r), 0)
        placed = placed + left(placed, -32)
        placed = placed + left(placed, -64) + chunk_of
        pb[r] = jnp.where(iota((512, 128), 0) == placed, 1.0, 0.0).astype(bf16)
    row = iota((512, 256), 0)
    col = iota((512, 256), 1)
    same = ((row >> 4) & 7) == ((col >> 4) & 7)
    k0, r, kind = row & 15, col & 15, row >> 7
    inside = jnp.where(
        kind == 0, (r >= k0).astype(i32),
        jnp.where(kind == 1, 1, jnp.where(kind == 2, (r < k0 + 12).astype(i32), (r < k0 - 4).astype(i32))))
    windows[...] = jnp.where(same, inside, 0).astype(f32).astype(bf16)

    pltpu.make_async_copy(send_a.at[pl.ds(0, NT - 1)], recv_a.at[pl.ds(0, NT - 1)], ra).wait()
    zf[...] = recv_a[...].astype(f32).reshape(512, 128)

    def pair(rr, _):
        z0[...] = jnp.concatenate([zf[pl.ds(4 * rr + bh, NT, stride=16), :] for bh in range(4)], axis=0).T

        z = z0[...]
        hi, lo = split2(z * z)
        sums = dot(windows[...], jnp.concatenate([hi, lo], axis=0))
        suffix, whole, e1, e2 = (sums[128 * i:128 * i + 128] for i in range(4))
        b2 = whole + next_block(whole)
        b4 = b2 + left(b2, 1)
        b8 = b4 + left(b4, 2)
        b16 = b8 + left(b8, 4)
        power = suffix + left(e1, 9) + next_block(b16 + left(whole, 8) + left(e2, 9))
        v = lax.rsqrt(power / TAPS + EPS)
        parts = [split2(x) for x in (v, next_block(v), left(v, 1))]
        blank = jnp.zeros((16, 128), bf16)

        lane16 = iota((16, 128), 1)
        pieces = [[None, None] for _ in range(4)]
        for s2 in range(2):
            s = rr * 2 + s2
            columns = []
            for c in range(3):
                at = 16 * (3 * s2 + c)
                columns.append(jnp.concatenate(
                    [x for part in range(2) for x in
                     [parts[e][part][at:at + 16] for e in range(3)] + [blank]], axis=0))
            norm = dot(tsel[s], jnp.concatenate(columns, axis=1))
            total = None
            for c in range(3):
                sc = s * 3 + c
                z = z0[16 * (3 * s2 + c):16 * (3 * s2 + c) + 16, :]
                z1 = next_block(z)
                lagged = jnp.concatenate(
                    [left(x, u) for u in range(12) for x in (z, z1)], axis=0).astype(bf16)
                numer = dot(wt[sc], lagged)
                scaled = norm[:, 128 * c:128 * c + 128].reshape(16, 16, 128) * invw[sc][:, None, :]
                term = numer.reshape(16, 16, 128) * scaled
                total = term if total is None else total + term
            ssc[s2] = total.reshape(256, 128)
            coarse = pk[pl.ds(pl.multiple_of(s * 16, 16), 16), :] >> 16
            for chunk in range(4):
                merged = None
                for low in range(4):
                    x = ssc[s2, pl.ds(4 * chunk + low, 16, stride=16), :]
                    for bit in range(4):
                        x = jnp.where((coarse & (1 << bit)) != 0, left(x, 1 << bit), x)
                    x = left(x, -8 * low)
                    merged = x if merged is None else jnp.where(((lane16 >> 3) & 3) == low, x, merged)
                pieces[chunk][s2] = merged
        corr = jnp.concatenate([x for two in pieces for x in two], axis=0).astype(bf16)
        send_b[rr] = dot(pb[rr], corr).astype(bf16).reshape(NT, 16, 128)
        recv_b[rr, me_t] = send_b[rr, me_t]

        def send_second(j, _):
            peer = tmpl_peer(me_t, j)
            pltpu.make_async_remote_copy(
                src_ref=send_b.at[rr, peer], dst_ref=recv_b.at[rr, me_t], send_sem=sb.at[rr], recv_sem=rb.at[rr],
                device_id={"tmpl": peer}, device_id_type=MESH).start()
            return 0

        lax.fori_loop(0, NT - 1, send_second, 0)
        return 0

    lax.fori_loop(0, 3, pair, 0)

    lane32 = iota((1, 128), 1)
    for rr in range(3):
        marks = zf[pl.ds(12 + rr, NT, stride=16), :]
        for u in range(4):
            mark = jnp.sum(marks[8 * u:8 * u + 8], axis=0, keepdims=True).astype(i32)
            key[4 * rr + u:4 * rr + u + 1, :] = jnp.where(mark > 0, (lane32 & 3) * 256 + mark - 1, -1)

    def onehot(n, _):
        line = iota((64, 128), 0)
        code = ((line >> 4) & 3) * 256 + (line & 15) + n * 16
        found = None
        start = pl.multiple_of(n * 64, 64)
        for rr in range(3):
            for u in range(4):
                hit = jnp.where(code == key[4 * rr + u:4 * rr + u + 1, :], 1.0, 0.0)
                ob[rr, pl.ds(start, 64), 128 * u:128 * u + 128] = hit.astype(bf16)
                found = hit[:16] if found is None else found + hit[:16]
        number = jnp.broadcast_to(jnp.sum(found, axis=1, keepdims=True), (16, 128)).astype(i32)
        parts = jnp.where(iota((16, 128), 1) < 64, number & 127, number >> 7)
        send_k[n] = parts.astype(f32).astype(bf16)
        return 0

    lax.fori_loop(0, NS, onehot, 0)
    recv_k[me_n] = send_k[me_n]

    def send_counts(j, _):
        peer = stn_peer(me_n, j)
        pltpu.make_async_remote_copy(
            src_ref=send_k.at[peer], dst_ref=recv_k.at[me_n], send_sem=sk, recv_sem=rk,
            device_id={"stn": peer}, device_id_type=MESH).start()
        return 0

    lax.fori_loop(0, NS - 1, send_counts, 0)

    k = iota((512, 512), 1)
    place = ((k >> 2) & 3) * 128 + (k >> 8) * 64 + ((k >> 4) & 1) * 32 + (k & 3) * 8 + ((k >> 5) & 7)
    q[...] = jnp.where(iota((512, 512), 0) == place, 1.0, 0.0).astype(bf16)

    for rr in range(2):
        pltpu.make_async_copy(send_b.at[rr, pl.ds(0, NT - 1)], recv_b.at[rr, pl.ds(0, NT - 1)], rb.at[rr]).wait()
        part = dot(ob[rr], recv_b[rr].reshape(512, 128))
        if rr == 0:
            acc[...] = part
        else:
            acc[...] += part
    pltpu.make_async_copy(send_b.at[2, pl.ds(0, NT - 1)], recv_b.at[2, pl.ds(0, NT - 1)], rb.at[2]).wait()
    last = recv_b[2].reshape(512, 128)
    for i in range(4):
        y = ((me_n >> 3) + 1 + i) & 1
        z = (((me_n >> 2) & 1) + 1 + (i >> 1)) & 1
        quarter = y * 2 + z
        rows = pl.ds(pl.multiple_of(quarter * 256, 256), 256)
        part = acc[rows, :] + dot(ob[2, rows, :], last)
        send_c[pl.ds(quarter * 4, 4)] = part.astype(bf16).reshape(4, 64, 128)

        def send_stacks(j, _):
            peer = quarter * 4 + ((me_n + j) & 3)
            pltpu.make_async_remote_copy(
                src_ref=send_c.at[peer], dst_ref=recv_c.at[me_n], send_sem=sc_, recv_sem=rc,
                device_id={"stn": peer}, device_id_type=MESH).start()
            return 0

        lax.fori_loop(1 if i == 3 else 0, 4, send_stacks, 0)
    recv_c[me_n] = send_c[me_n]

    pltpu.make_async_copy(send_k.at[pl.ds(0, NS - 1)], recv_k.at[pl.ds(0, NS - 1)], rk).wait()
    found = jnp.sum(recv_k[...].astype(f32), axis=0)
    found = jnp.where(iota((16, 128), 1) < 64, found, found * 128.0)
    found = found + left(found, 64)
    scale = jnp.sqrt(f32(TAPS)) * lax.rsqrt(jnp.maximum(found, 1.0))

    pltpu.make_async_copy(send_c.at[pl.ds(0, NS - 1)], recv_c.at[pl.ds(0, NS - 1)], rc).wait()
    y = jnp.sum(recv_c[...].astype(f32), axis=0).reshape(4, 16, 128) * scale[None]
    y = jnp.concatenate([y[0], y[1], y[2], y[3]], axis=1)
    hi, rest = y.astype(bf16), y - y.astype(bf16).astype(f32)
    mid, low = split2(rest)
    moved = dot(jnp.concatenate([hi, mid, low], axis=0), q[...])
    moved = moved[0:16] + moved[16:32] + moved[32:48]
    out[0] = moved[:, :256]
    out[1] = moved[:, 256:]

    pltpu.make_async_copy(send_a.at[pl.ds(0, NT - 1)], recv_a.at[pl.ds(0, NT - 1)], sa).wait()
    for rr in range(3):
        pltpu.make_async_copy(send_b.at[rr, pl.ds(0, NT - 1)], recv_b.at[rr, pl.ds(0, NT - 1)], sb.at[rr]).wait()
    pltpu.make_async_copy(send_k.at[pl.ds(0, NS - 1)], recv_k.at[pl.ds(0, NS - 1)], sk).wait()
    pltpu.make_async_copy(send_c.at[pl.ds(0, NS - 1)], recv_c.at[pl.ds(0, NS - 1)], sc_).wait()


def body(data, waves, slot_group, slot_local, moveout, chan_mask):
    vmem = pl.BlockSpec(memory_space=pltpu.VMEM)
    hbm = pl.BlockSpec(memory_space=pltpu.HBM)
    dma = pltpu.SemaphoreType.DMA
    return pl.pallas_call(
        kernel,
        out_shape=jax.ShapeDtypeStruct((2, 16, 256), f32),
        in_specs=[hbm] * 6,
        out_specs=vmem,
        scratch_shapes=[
            pltpu.VMEM((24, 2, 32), bf16),
            pltpu.VMEM((18, 16, TAPS), bf16),
            pltpu.VMEM((6, 1, 16), i32),
            pltpu.VMEM((6, 16), i32),
            pltpu.VMEM((6, 16), i32),
            pltpu.SMEM((3, 6), i32),
            pltpu.VMEM((96, 128), i32),
            pltpu.VMEM((8, 128), i32),
            pltpu.VMEM((NT, 16, 128), bf16),
            pltpu.VMEM((NT, 16, 128), bf16),
            pltpu.VMEM((18, 256, 384), bf16),
            pltpu.VMEM((18, 16, 128), f32),
            pltpu.VMEM((6, 256, 128), bf16),
            pltpu.VMEM((3, 512, 128), bf16),
            pltpu.VMEM((512, 256), bf16),
            pltpu.VMEM((128, 128), f32),
            pltpu.VMEM((512, 128), f32),
            pltpu.VMEM((2, 256, 128), f32),
            pltpu.VMEM((3, NT, 16, 128), bf16),
            pltpu.VMEM((3, NT, 16, 128), bf16),
            pltpu.VMEM((16, 128), i32),
            pltpu.VMEM((3, 1024, 512), bf16),
            pltpu.VMEM((1024, 128), f32),
            pltpu.VMEM((NS, 64, 128), bf16),
            pltpu.VMEM((NS, 64, 128), bf16),
            pltpu.VMEM((NS, 16, 128), bf16),
            pltpu.VMEM((NS, 16, 128), bf16),
            pltpu.VMEM((512, 512), bf16),
            dma((5,)), dma, dma, dma, dma((3,)), dma((3,)), dma, dma, dma, dma,
        ],
        compiler_params=pltpu.CompilerParams(
            collective_id=0, has_side_effects=True, vmem_limit_bytes=60 * 2**20),
    )(
        jnp.transpose(data, (1, 2, 0, 3)).reshape(18, 2, 32),
        jnp.transpose(waves, (0, 2, 1, 3)).reshape(18, 16, TAPS),
        jnp.transpose(slot_group, (0, 2, 1)),
        slot_local, moveout, jnp.transpose(chan_mask),
    )


def solution(mesh):
    in_specs = (
        P(None, "stn", None, "tmpl"),
        P("stn", "tmpl", None, None),
        P("stn", "tmpl", None),
        P("stn", "tmpl"),
        P("stn", "tmpl"),
        P("stn", None),
    )
    out_specs = P(None, ("tmpl", "stn"), None)
    return jax.shard_map(body, mesh=mesh, in_specs=in_specs, out_specs=out_specs, check_vma=False)
```

```python
import functools

import jax
import jax.numpy as jnp
from jax import lax
from jax.experimental import pallas as pl
from jax.experimental.pallas import tpu as pltpu
from jax.sharding import PartitionSpec as P

NT = 32
NS = 16
TAPS = 300
EPS = 1e-06
MESH = pl.DeviceIdType.MESH
f32, bf16, i32 = jnp.float32, jnp.bfloat16, jnp.int32


def iota(shape, axis):
    return lax.broadcasted_iota(i32, shape, axis)


def left(x, by):
    by %= 128
    return x if by == 0 else pltpu.roll(x, 128 - by, axis=x.ndim - 1)


def next_block(x):
    half = (iota(x.shape, x.ndim - 1) >> 5) & 1
    return jnp.where(half == 0, left(x, 32), left(x, -31))


def split2(x):
    hi = x.astype(bf16)
    return hi, (x - hi.astype(f32)).astype(bf16)


def dot(a, b):
    return jnp.dot(a, b, preferred_element_type=f32)


def far_first(j):
    return jnp.where(j < 2, 2 - j, 9 - 3 * j)


def tmpl_peer(me, j):
    y = far_first(j >> 3)
    x = far_first((j >> 1) & 3)
    return ((((me >> 3) + x) & 3) << 3) | ((((me >> 1) + y) & 3) << 1) | ((me + 1 + j) & 1)


def stn_peer(me, j):
    a = j >> 1
    z = jnp.where((a & 1) == 1, 4 - ((a + 1) >> 1), 4 + (a >> 1))
    return ((((me >> 3) + 1 + j) & 1) << 3) | ((me + z) & 7)


def kernel(
    data_in, waves_in, group_in, local_in, move_in, mask_in, out,
    data_v, w0, group_v, local_v, move_v, cm, pk, codes,
    send_a, recv_a, wt, invw, tsel, pb, windows, z0, zf, ssc, aligned, vb,
    send_b, recv_b, key, ob, acc, send_c, recv_c, send_k, recv_k, q,
    si, sw, sa, ra, sb, rb, sc_, rc, sk, rk,
):
    me_t, me_n = lax.axis_index("tmpl"), lax.axis_index("stn")
    small = [
        pltpu.make_async_copy(data_in, data_v.at[pl.ds(0, 18)], si.at[0]),
        pltpu.make_async_copy(group_in, group_v, si.at[1]),
        pltpu.make_async_copy(local_in, local_v, si.at[2]),
        pltpu.make_async_copy(move_in, move_v, si.at[3]),
        pltpu.make_async_copy(mask_in, cm, si.at[4]),
    ]
    large = pltpu.make_async_copy(waves_in, w0, sw)
    for copy in small:
        copy.start()
    large.start()

    bar = pltpu.get_barrier_semaphore()

    def greet_t(j, _):
        pl.semaphore_signal(bar, inc=1, device_id={"tmpl": tmpl_peer(me_t, j)}, device_id_type=MESH)
        return 0

    def greet_n(j, _):
        pl.semaphore_signal(bar, inc=1, device_id={"stn": stn_peer(me_n, j)}, device_id_type=MESH)
        return 0

    lax.fori_loop(0, NT - 1, greet_t, 0)
    lax.fori_loop(0, NS - 1, greet_n, 0)
    for copy in small:
        copy.wait()

    sub16, lane16s = iota((16, 16), 0), iota((16, 16), 1)
    codes[...] = jnp.zeros((8, 128), i32)
    for s in range(6):
        group = jnp.broadcast_to(group_v[s], (16, 16))
        column = jnp.sum(jnp.where(sub16 == lane16s, group, 0).astype(f32), axis=1, keepdims=True).astype(i32)
        same = group == column
        rank_rows = jnp.sum(jnp.where(same & (lane16s < sub16), 1.0, 0.0), axis=1, keepdims=True)
        rank_lanes = jnp.sum(jnp.where(same & (sub16 < lane16s), 1.0, 0.0), axis=0, keepdims=True)
        fields = (move_v[s:s + 1, :] << 11) | ((local_v[s:s + 1, :] + 1) << 2) | ((s & 1) * 2)
        fields = jnp.where(sub16 == lane16s, jnp.broadcast_to(fields, (16, 16)), 0)
        fields = jnp.sum(fields.astype(f32), axis=1, keepdims=True) + rank_rows
        pk[16 * s:16 * s + 16, :] = jnp.broadcast_to(fields, (16, 128)).astype(i32)
        codes[s:s + 1, 0:16] = group_v[s] * 16 + ((s & 1) * 2 + rank_lanes.astype(i32)) * 4
    spread = pltpu.roll(codes[...].astype(f32), 0, axis=1, stride=16, stride_axis=0)
    code = jnp.sum(spread, axis=0, keepdims=True).astype(i32)

    parts = []
    row24, lane24 = iota((24, 128), 0), iota((24, 128), 1)
    third = (row24 >= 6).astype(i32) + (row24 >= 12).astype(i32)
    keep = ((lane24 >> 4) == row24 - 6 * third) & (row24 < 18)
    for b in range(2):
        samples = data_v[:, b, :]
        for half in range(2):
            widen = iota((32, 128), 0) == half * 16 + (iota((32, 128), 1) & 15)
            parts.append(jnp.where(keep, dot(samples, jnp.where(widen, 1.0, 0.0).astype(bf16)), 0.0))
    source = iota((16, 128), 1)
    dest = iota((16, 128), 0)
    bh = (source >= 24).astype(i32) + (source >= 48).astype(i32) + (source >= 72).astype(i32)
    sc24 = source - 24 * bh
    gather = dest == ((sc24 >= 6).astype(i32) + (sc24 >= 12).astype(i32)) * 4 + bh
    gather = jnp.where(gather & (sc24 < 18) & (source < 96), 1.0, 0.0).astype(bf16)
    stacked = jnp.concatenate(parts + [jnp.zeros((32, 128), f32)], axis=0).astype(bf16)
    dtile = dot(gather, stacked)
    lane = iota((96, 128), 1)
    packed = pk[...]
    mine = (lane >> 4) == (me_t & 7)
    pair_of = iota((96, 128), 0) >> 5
    spot = jnp.where(pair_of == 0, (lane & 15) >> 2, ((lane & 15) >> 1) + 4 - 4 * pair_of)
    id_rows = jnp.where(mine & (spot == (packed & 3)), (packed >> 2) & 511, 0)
    first = (code & -16) + 12 + (iota((1, 128), 1) >= 32).astype(i32)
    pick = iota((512, 96), 0) == first[:, 0:96]
    ids = dot(jnp.where(pick, 1.0, 0.0).astype(bf16), id_rows.astype(f32).astype(bf16))
    send_a[...] = (ids.reshape(NT, 16, 128) + dtile[None]).astype(bf16)
    recv_a[me_t] = send_a[me_t]

    pl.semaphore_wait(bar, NT - 1 + NS - 1)

    def send_first(j, _):
        peer = tmpl_peer(me_t, j)
        pltpu.make_async_remote_copy(
            src_ref=send_a.at[peer], dst_ref=recv_a.at[me_t], send_sem=sa, recv_sem=ra,
            device_id={"tmpl": peer}, device_id_type=MESH).start()
        return 0

    lax.fori_loop(0, NT - 1, send_first, 0)

    large.wait()

    def prepare(s, _):
        rows = pk[pl.ds(pl.multiple_of(s * 16, 16), 16), :]
        fine = (rows >> 11) & 31
        lane16 = iota((16, 128), 1)
        usable = [cm[c, s].astype(f32) for c in range(3)]
        total = usable[0] + usable[1] + usable[2]
        per = jnp.where(total > 2.5, 1.0 / 3.0, jnp.where(total > 1.5, 0.5, 1.0)) / TAPS
        for c in range(3):
            sc = s * 3 + c
            x = [w0[sc, :, 0:128].astype(f32), w0[sc, :, 128:256].astype(f32),
                 jnp.pad(w0[sc, :, 256:TAPS].astype(f32), ((0, 0), (0, 384 - TAPS)))]
            power = jnp.sum(x[0] * x[0] + x[1] * x[1] + x[2] * x[2], axis=1, keepdims=True)
            invw[sc] = jnp.broadcast_to(lax.rsqrt(power / TAPS + EPS), (16, 128)) * (usable[c] * per)
            for bit in range(5):
                by = 1 << bit
                y = [pltpu.roll(v, by, axis=1) for v in x]
                wide = [jnp.where(lane16 >= by, y[j], y[j - 1] if j else 0.0) for j in range(3)]
                on = (fine & by) != 0
                x = [jnp.where(on, wide[j], x[j]) for j in range(3)]
            k0 = iota((16, 16, 128), 1)
            l3 = iota((16, 16, 128), 2)
            y = [
                pltpu.roll(jnp.broadcast_to(v[:, None, :], (16, 16, 128)), 0, axis=2, stride=1, stride_axis=1)
                for v in x
            ]
            for j in range(3):
                t = jnp.where(l3 >= k0, y[j], y[j - 1] if j else 0.0)
                wt[sc, :, 128 * j:128 * j + 128] = t.reshape(256, 128).astype(bf16)
        k0 = iota((16, 16, 128), 1)
        l3 = iota((16, 16, 128), 2)
        hit = (l3 & 63) == k0 + fine[:, None, :]
        tsel[s] = jnp.where(hit, 1.0, 0.0).reshape(256, 128).astype(bf16)
        return 0

    lax.fori_loop(0, 6, prepare, 0)

    lane1 = iota((1, 128), 1)
    placed = jnp.where(lane1 < 32, code, 0)
    placed = placed + left(placed, -32)
    placed = placed + left(placed, -64) + (lane1 >> 5)
    pb[0] = jnp.where(iota((512, 128), 0) == placed, 1.0, 0.0).astype(bf16)
    later = left(code, 32)
    placed = jnp.where(lane1 < 64, (later & -16) + (lane1 >> 5) * 8 + ((later >> 2) & 3) * 2, 0)
    placed = placed + left(placed, -64) + (lane1 >> 6)
    pb[1] = jnp.where(iota((512, 128), 0) == placed, 1.0, 0.0).astype(bf16)
    row = iota((288, 256), 0)
    col = iota((288, 256), 1)
    kind = (row >= 96).astype(i32) + (row >= 192).astype(i32)
    row = row - 96 * kind
    k0, r = row & 15, col & 15
    inside = jnp.where(
        kind == 0, (r >= k0).astype(i32), jnp.where(kind == 1, (r < k0 + 12).astype(i32), (r < k0 - 4).astype(i32)))
    same = (row >> 4) == ((col >> 4) & 7)
    windows[0:288, :] = jnp.where(same, inside, 0).astype(f32).astype(bf16)
    same = iota((16, 256), 0) == ((iota((16, 256), 1) >> 4) & 7)
    windows[288:304, :] = jnp.where(same, 1.0, 0.0).astype(bf16)

    vb[:, 48:64, :] = jnp.zeros((6, 16, 384), bf16)
    vb[:, 112:128, :] = jnp.zeros((6, 16, 384), bf16)

    pltpu.make_async_copy(send_a.at[pl.ds(0, NT - 1)], recv_a.at[pl.ds(0, NT - 1)], ra).wait()
    zf[...] = recv_a[...].astype(f32).reshape(512, 128)

    sums = []
    for rr in range(3):
        z = jnp.concatenate([zf[pl.ds(4 * rr + bh, NT, stride=16), :] for bh in range(4)], axis=0).T
        z0[rr] = z
        hi, lo = split2(z * z)
        sums.append(dot(windows[...], jnp.concatenate([hi, lo], axis=0)))
    suffix, e1, e2 = (jnp.concatenate([x[96 * i:96 * i + 96] for x in sums], axis=0) for i in range(3))
    whole = jnp.concatenate([x[288:296] for x in sums], axis=0)
    b2 = whole + next_block(whole)
    b4 = b2 + left(b2, 1)
    b8 = b4 + left(b4, 2)
    b16 = b8 + left(b8, 4)
    middle = next_block(b16 + left(whole, 8))
    middle = jnp.concatenate(
        [jnp.broadcast_to(middle[8 * rr + k:8 * rr + k + 1], (16, 128)) for rr in range(3) for k in range(6)], axis=0)
    half = (iota((288, 128), 1) >> 5) & 1
    power = suffix + left(e1, 9) + (middle + jnp.where(half == 0, left(e2, 41), left(e2, -22)))
    v = lax.rsqrt(power / TAPS + EPS)
    for e, x in enumerate((v, next_block(v), left(v, 1))):
        for part, y in enumerate(split2(x)):
            for sc in range(18):
                at = 64 * part + 16 * e
                vb[sc // 3, at:at + 16, 128 * (sc % 3):128 * (sc % 3) + 128] = y[16 * sc:16 * sc + 16]

    def pair(rr, _):
        lane16 = iota((16, 128), 1)
        for s2 in range(2):
            s = rr * 2 + s2
            norm = dot(tsel[s], vb[s])
            total = None
            for c in range(3):
                sc = s * 3 + c
                z = z0[rr, 16 * (3 * s2 + c):16 * (3 * s2 + c) + 16, :]
                z1 = next_block(z).astype(bf16)
                z = z.astype(bf16)
                lagged = jnp.concatenate([left(x, u) for u in range(12) for x in (z, z1)], axis=0)
                numer = dot(wt[sc], lagged)
                scaled = norm[:, 128 * c:128 * c + 128].reshape(16, 16, 128) * invw[sc][:, None, :]
                term = numer.reshape(16, 16, 128) * scaled
                total = term if total is None else total + term
            ssc[s] = total.reshape(256, 128)
            coarse = pk[pl.ds(pl.multiple_of(16 * s, 16), 16), :] >> 16
            for chunk in range(4):
                merged = None
                for low in range(4):
                    x = ssc[s, pl.ds(4 * chunk + low, 16, stride=16), :].astype(bf16)
                    for bit in range(4):
                        x = jnp.where((coarse & (1 << bit)) != 0, left(x, 1 << bit), x)
                    x = left(x, -8 * low)
                    merged = x if merged is None else jnp.where(((lane16 >> 3) & 3) == low, x, merged)
                aligned[chunk, pl.ds(pl.multiple_of(16 * s, 16), 16), :] = merged
        return 0

    def send(k, which, rows):
        corr = jnp.concatenate(rows, axis=0)
        send_b[k] = dot(pb[which], corr).astype(bf16).reshape(NT, 16, 128)

        def send_second(j, _):
            peer = tmpl_peer(me_t, j)
            pltpu.make_async_remote_copy(
                src_ref=send_b.at[k, peer], dst_ref=recv_b.at[k, me_t], send_sem=sb.at[k], recv_sem=rb.at[k],
                device_id={"tmpl": peer}, device_id_type=MESH).start()
            return 0

        for j in range(NT - 1):
            send_second(j, 0)
        recv_b[k, me_t] = send_b[k, me_t]

    lax.fori_loop(0, 1, pair, 0)
    send(0, 0, [aligned[c, 0:32, :] for c in range(4)])
    lax.fori_loop(1, 3, pair, 0)
    for k in range(2):
        send(1 + k, 1, [aligned[c, 32:96, :] for c in (2 * k, 2 * k + 1)])

    for k in range(2):
        marks = zf[pl.ds(12 + k, NT, stride=16), :]
        for u in range(4):
            mark = jnp.sum(marks[8 * u:8 * u + 8], axis=0, keepdims=True).astype(i32)
            chunk = lane1 & (1 if k else 3)
            key[4 * k + u:4 * k + u + 1, :] = jnp.where(mark > 0, chunk * 256 + mark - 1, -1)

    def onehot(n, _):
        line = iota((64, 128), 0)
        code = (line >> 4) * 256 + (line & 15) + n * 16
        found = None
        rows = pl.ds(pl.multiple_of(n * 32, 32), 32)
        for u in range(4):
            at = slice(128 * u, 128 * u + 128)
            hit = jnp.where(code == key[u:u + 1, :], 1.0, 0.0)
            ob[0, rows, at] = hit[:32].astype(bf16)
            ob[1, rows, at] = hit[32:].astype(bf16)
            found = hit[:16] if found is None else found + hit[:16]
            hit = jnp.where(code[:32] == key[4 + u:5 + u, :], 1.0, 0.0)
            ob[2, rows, at] = hit.astype(bf16)
            found = found + hit[:16]
        number = jnp.broadcast_to(jnp.sum(found, axis=1, keepdims=True), (16, 128)).astype(i32)
        parts = jnp.where(iota((16, 128), 1) < 64, number & 127, number >> 7)
        send_k[n] = parts.astype(f32).astype(bf16)
        return 0

    lax.fori_loop(0, NS, onehot, 0)

    def send_counts(j, _):
        peer = stn_peer(me_n, j)
        pltpu.make_async_remote_copy(
            src_ref=send_k.at[peer], dst_ref=recv_k.at[me_n], send_sem=sk, recv_sem=rk,
            device_id={"stn": peer}, device_id_type=MESH).start()
        return 0

    lax.fori_loop(0, NS - 1, send_counts, 0)
    recv_k[me_n] = send_k[me_n]

    k = iota((512, 512), 1)
    place = ((k >> 2) & 3) * 128 + (k >> 8) * 64 + ((k >> 4) & 1) * 32 + (k & 3) * 8 + ((k >> 5) & 7)
    q[...] = jnp.where(iota((512, 512), 0) == place, 1.0, 0.0).astype(bf16)

    def arrived(k):
        pltpu.make_async_copy(send_b.at[k, pl.ds(0, NT - 1)], recv_b.at[k, pl.ds(0, NT - 1)], rb.at[k]).wait()
        return recv_b[k].reshape(512, 128)

    stations = arrived(0)
    for h in range(2):
        acc[h] = dot(ob[h], stations)
    for h in range(2):
        stations = arrived(1 + h)
        for i in range(2):
            y = ((me_n >> 3) + 1 + i) & 1
            rows = pl.ds(pl.multiple_of(y * 256, 256), 256)
            part = acc[h, rows, :] + dot(ob[2, rows, :], stations)
            send_c[h, pl.ds(y * 8, 8)] = part.astype(bf16).reshape(8, 32, 128)

            def send_stacks(a, _):
                z = jnp.where((a & 1) == 1, 4 - ((a + 1) >> 1), 4 + (a >> 1))
                peer = y * 8 + ((me_n + z) & 7)
                pltpu.make_async_remote_copy(
                    src_ref=send_c.at[h, peer], dst_ref=recv_c.at[h, me_n], send_sem=sc_.at[h], recv_sem=rc.at[h],
                    device_id={"stn": peer}, device_id_type=MESH).start()
                return 0

            lax.fori_loop(0, 7 if i == 1 else 8, send_stacks, 0)
        recv_c[h, me_n] = send_c[h, me_n]

    pltpu.make_async_copy(send_k.at[pl.ds(0, NS - 1)], recv_k.at[pl.ds(0, NS - 1)], rk).wait()
    found = jnp.sum(recv_k[...].astype(f32), axis=0)
    found = jnp.where(iota((16, 128), 1) < 64, found, found * 128.0)
    found = found + left(found, 64)
    scale = jnp.sqrt(f32(TAPS)) * lax.rsqrt(jnp.maximum(found, 1.0))

    ordered = []
    for h in range(2):
        pltpu.make_async_copy(send_c.at[h, pl.ds(0, NS - 1)], recv_c.at[h, pl.ds(0, NS - 1)], rc.at[h]).wait()
        y = jnp.sum(recv_c[h].astype(f32), axis=0)
        ordered += [y[:16] * scale, y[16:] * scale]
    y = jnp.concatenate(ordered, axis=1)
    hi, rest = y.astype(bf16), y - y.astype(bf16).astype(f32)
    mid, low = split2(rest)
    moved = dot(jnp.concatenate([hi, mid, low], axis=0), q[...])
    moved = moved[0:16] + moved[16:32] + moved[32:48]
    out[0] = moved[:, :256]
    out[1] = moved[:, 256:]

    pltpu.make_async_copy(send_a.at[pl.ds(0, NT - 1)], recv_a.at[pl.ds(0, NT - 1)], sa).wait()
    for rr in range(3):
        pltpu.make_async_copy(send_b.at[rr, pl.ds(0, NT - 1)], recv_b.at[rr, pl.ds(0, NT - 1)], sb.at[rr]).wait()
    pltpu.make_async_copy(send_k.at[pl.ds(0, NS - 1)], recv_k.at[pl.ds(0, NS - 1)], sk).wait()
    for h in range(2):
        pltpu.make_async_copy(send_c.at[h, pl.ds(0, NS - 1)], recv_c.at[h, pl.ds(0, NS - 1)], sc_.at[h]).wait()


def body(data, waves, slot_group, slot_local, moveout, chan_mask):
    vmem = pl.BlockSpec(memory_space=pltpu.VMEM)
    hbm = pl.BlockSpec(memory_space=pltpu.HBM)
    dma = pltpu.SemaphoreType.DMA
    return pl.pallas_call(
        kernel,
        out_shape=pltpu.VMEM((2, 16, 256), f32),
        in_specs=[hbm] * 6,
        out_specs=vmem,
        scratch_shapes=[
            pltpu.VMEM((24, 2, 32), bf16),
            pltpu.VMEM((18, 16, TAPS), bf16),
            pltpu.VMEM((6, 1, 16), i32),
            pltpu.VMEM((6, 16), i32),
            pltpu.VMEM((6, 16), i32),
            pltpu.SMEM((3, 6), i32),
            pltpu.VMEM((96, 128), i32),
            pltpu.VMEM((8, 128), i32),
            pltpu.VMEM((NT, 16, 128), bf16),
            pltpu.VMEM((NT, 16, 128), bf16),
            pltpu.VMEM((18, 256, 384), bf16),
            pltpu.VMEM((18, 16, 128), f32),
            pltpu.VMEM((6, 256, 128), bf16),
            pltpu.VMEM((2, 512, 128), bf16),
            pltpu.VMEM((304, 256), bf16),
            pltpu.VMEM((3, 128, 128), f32),
            pltpu.VMEM((512, 128), f32),
            pltpu.VMEM((6, 256, 128), f32),
            pltpu.VMEM((4, 96, 128), bf16),
            pltpu.VMEM((6, 128, 384), bf16),
            pltpu.VMEM((3, NT, 16, 128), bf16),
            pltpu.VMEM((3, NT, 16, 128), bf16),
            pltpu.VMEM((16, 128), i32),
            pltpu.VMEM((3, 512, 512), bf16),
            pltpu.VMEM((2, 512, 128), f32),
            pltpu.VMEM((2, NS, 32, 128), bf16),
            pltpu.VMEM((2, NS, 32, 128), bf16),
            pltpu.VMEM((NS, 16, 128), bf16),
            pltpu.VMEM((NS, 16, 128), bf16),
            pltpu.VMEM((512, 512), bf16),
            dma((5,)), dma, dma, dma, dma((3,)), dma((3,)), dma((2,)), dma((2,)), dma, dma,
        ],
        compiler_params=pltpu.CompilerParams(
            collective_id=0, has_side_effects=True, vmem_limit_bytes=60 * 2**20),
    )(
        jnp.transpose(data, (1, 2, 0, 3)).reshape(18, 2, 32),
        jnp.transpose(waves, (0, 2, 1, 3)).reshape(18, 16, TAPS),
        jnp.transpose(slot_group, (0, 2, 1)),
        slot_local, moveout, jnp.transpose(chan_mask),
    )


def solution(mesh):
    in_specs = (
        P(None, "stn", None, "tmpl"),
        P("stn", "tmpl", None, None),
        P("stn", "tmpl", None),
        P("stn", "tmpl"),
        P("stn", "tmpl"),
        P("stn", None),
    )
    out_specs = P(None, ("tmpl", "stn"), None)
    return jax.shard_map(body, mesh=mesh, in_specs=in_specs, out_specs=out_specs, check_vma=False)
```

```python
import functools

import jax
import jax.numpy as jnp
from jax import lax
from jax.experimental import pallas as pl
from jax.experimental.pallas import tpu as pltpu
from jax.sharding import PartitionSpec as P

NT = 32
NS = 16
TAPS = 300
EPS = 1e-06
MESH = pl.DeviceIdType.MESH
f32, bf16, i32 = jnp.float32, jnp.bfloat16, jnp.int32


def iota(shape, axis):
    return lax.broadcasted_iota(i32, shape, axis)


def left(x, by):
    by %= 128
    return x if by == 0 else pltpu.roll(x, 128 - by, axis=x.ndim - 1)


def next_block(x):
    half = (iota(x.shape, x.ndim - 1) >> 5) & 1
    return jnp.where(half == 0, left(x, 32), left(x, -31))


def split2(x):
    hi = x.astype(bf16)
    return hi, (x - hi.astype(f32)).astype(bf16)


def dot(a, b):
    return jnp.dot(a, b, preferred_element_type=f32)


def around(step, size):
    return min(step, size - step)


TMPL = sorted(
    ((x, y, c) for x in range(4) for y in range(4) for c in range(2) if x or y or c),
    key=lambda d: -(around(d[0], 4) + 2 * around(d[1], 4) + 0.5 * d[2]))
STN = sorted(
    ((y, z) for y in range(2) for z in range(8) if y or z), key=lambda d: -(d[0] + around(d[1], 8)))


def tmpl_peer(me, by):
    x, y, c = by
    return ((((me >> 3) + x) & 3) << 3) | ((((me >> 1) + y) & 3) << 1) | ((me + c) & 1)


def stn_peer(me, by):
    y, z = by
    return ((((me >> 3) + y) & 1) << 3) | ((me + z) & 7)


def kernel(
    data_in, waves_in, group_in, local_in, move_in, mask_in, out,
    data_v, w0, group_v, local_v, move_v, cm, pk, codes,
    send_a, recv_a, wt, invw, tsel, pb, windows, z0, zf, ssc, aligned, vb,
    send_b, recv_b, key, ob, acc, send_c, recv_c, send_k, recv_k, q,
    si, sw, sa, ra, sb, rb, sc_, rc, sk, rk,
):
    me_t, me_n = lax.axis_index("tmpl"), lax.axis_index("stn")
    small = [
        pltpu.make_async_copy(data_in, data_v.at[pl.ds(0, 18)], si.at[0]),
        pltpu.make_async_copy(group_in, group_v, si.at[1]),
        pltpu.make_async_copy(local_in, local_v, si.at[2]),
        pltpu.make_async_copy(move_in, move_v, si.at[3]),
        pltpu.make_async_copy(mask_in, cm, si.at[4]),
    ]
    large = pltpu.make_async_copy(waves_in, w0, sw)
    for copy in small:
        copy.start()
    large.start()

    bar = pltpu.get_barrier_semaphore()

    for by in sorted(TMPL + STN, key=lambda d: -(
            around(d[0], 4) + 2 * around(d[1], 4) if len(d) == 3 else d[0] + around(d[1], 8))):
        to = {"tmpl": tmpl_peer(me_t, by)} if len(by) == 3 else {"stn": stn_peer(me_n, by)}
        pl.semaphore_signal(bar, inc=1, device_id=to, device_id_type=MESH)
    for copy in small:
        copy.wait()

    sub16, lane16s = iota((16, 16), 0), iota((16, 16), 1)
    codes[...] = jnp.zeros((8, 128), i32)
    for s in range(6):
        group = jnp.broadcast_to(group_v[s], (16, 16))
        column = jnp.sum(jnp.where(sub16 == lane16s, group, 0).astype(f32), axis=1, keepdims=True).astype(i32)
        same = group == column
        rank_rows = jnp.sum(jnp.where(same & (lane16s < sub16), 1.0, 0.0), axis=1, keepdims=True)
        rank_lanes = jnp.sum(jnp.where(same & (sub16 < lane16s), 1.0, 0.0), axis=0, keepdims=True)
        fields = (move_v[s:s + 1, :] << 11) | ((local_v[s:s + 1, :] + 1) << 2) | ((s & 1) * 2)
        fields = jnp.where(sub16 == lane16s, jnp.broadcast_to(fields, (16, 16)), 0)
        fields = jnp.sum(fields.astype(f32), axis=1, keepdims=True) + rank_rows
        pk[16 * s:16 * s + 16, :] = jnp.broadcast_to(fields, (16, 128)).astype(i32)
        codes[s:s + 1, 0:16] = group_v[s] * 16 + ((s & 1) * 2 + rank_lanes.astype(i32)) * 4
    spread = pltpu.roll(codes[...].astype(f32), 0, axis=1, stride=16, stride_axis=0)
    code = jnp.sum(spread, axis=0, keepdims=True).astype(i32)

    parts = []
    row24, lane24 = iota((24, 128), 0), iota((24, 128), 1)
    third = (row24 >= 6).astype(i32) + (row24 >= 12).astype(i32)
    keep = ((lane24 >> 4) == row24 - 6 * third) & (row24 < 18)
    for b in range(2):
        samples = data_v[:, b, :]
        for half in range(2):
            widen = iota((32, 128), 0) == half * 16 + (iota((32, 128), 1) & 15)
            parts.append(jnp.where(keep, dot(samples, jnp.where(widen, 1.0, 0.0).astype(bf16)), 0.0))
    source = iota((16, 128), 1)
    dest = iota((16, 128), 0)
    bh = (source >= 24).astype(i32) + (source >= 48).astype(i32) + (source >= 72).astype(i32)
    sc24 = source - 24 * bh
    gather = dest == ((sc24 >= 6).astype(i32) + (sc24 >= 12).astype(i32)) * 4 + bh
    gather = jnp.where(gather & (sc24 < 18) & (source < 96), 1.0, 0.0).astype(bf16)
    stacked = jnp.concatenate(parts + [jnp.zeros((32, 128), f32)], axis=0).astype(bf16)
    dtile = dot(gather, stacked)
    lane = iota((96, 128), 1)
    packed = pk[...]
    mine = (lane >> 4) == (me_t & 7)
    pair_of = iota((96, 128), 0) >> 5
    spot = jnp.where(pair_of == 0, (lane & 15) >> 2, ((lane & 15) >> 1) + 4 - 4 * pair_of)
    id_rows = jnp.where(mine & (spot == (packed & 3)), (packed >> 2) & 511, 0)
    first = (code & -16) + 12 + (iota((1, 128), 1) >= 32).astype(i32)
    pick = iota((512, 96), 0) == first[:, 0:96]
    ids = dot(jnp.where(pick, 1.0, 0.0).astype(bf16), id_rows.astype(f32).astype(bf16))
    send_a[...] = (ids.reshape(NT, 16, 128) + dtile[None]).astype(bf16)
    recv_a[me_t] = send_a[me_t]

    pl.semaphore_wait(bar, NT - 1 + NS - 1)

    for by in TMPL:
        peer = tmpl_peer(me_t, by)
        pltpu.make_async_remote_copy(
            src_ref=send_a.at[peer], dst_ref=recv_a.at[me_t], send_sem=sa, recv_sem=ra,
            device_id={"tmpl": peer}, device_id_type=MESH).start()

    large.wait()

    def prepare(s, _):
        rows = pk[pl.ds(pl.multiple_of(s * 16, 16), 16), :]
        fine = (rows >> 11) & 31
        lane16 = iota((16, 128), 1)
        usable = [cm[c, s].astype(f32) for c in range(3)]
        total = usable[0] + usable[1] + usable[2]
        per = jnp.where(total > 2.5, 1.0 / 3.0, jnp.where(total > 1.5, 0.5, 1.0)) / TAPS
        for c in range(3):
            sc = s * 3 + c
            x = [w0[sc, :, 0:128].astype(f32), w0[sc, :, 128:256].astype(f32),
                 jnp.pad(w0[sc, :, 256:TAPS].astype(f32), ((0, 0), (0, 384 - TAPS)))]
            power = jnp.sum(x[0] * x[0] + x[1] * x[1] + x[2] * x[2], axis=1, keepdims=True)
            invw[sc] = jnp.broadcast_to(lax.rsqrt(power / TAPS + EPS), (16, 128)) * (usable[c] * per)
            for bit in range(5):
                by = 1 << bit
                y = [pltpu.roll(v, by, axis=1) for v in x]
                wide = [jnp.where(lane16 >= by, y[j], y[j - 1] if j else 0.0) for j in range(3)]
                on = (fine & by) != 0
                x = [jnp.where(on, wide[j], x[j]) for j in range(3)]
            k0 = iota((16, 16, 128), 1)
            l3 = iota((16, 16, 128), 2)
            y = [
                pltpu.roll(jnp.broadcast_to(v[:, None, :], (16, 16, 128)), 0, axis=2, stride=1, stride_axis=1)
                for v in x
            ]
            for j in range(3):
                t = jnp.where(l3 >= k0, y[j], y[j - 1] if j else 0.0)
                wt[sc, :, 128 * j:128 * j + 128] = t.reshape(256, 128).astype(bf16)
        k0 = iota((16, 16, 128), 1)
        l3 = iota((16, 16, 128), 2)
        hit = (l3 & 63) == k0 + fine[:, None, :]
        tsel[s] = jnp.where(hit, 1.0, 0.0).reshape(256, 128).astype(bf16)
        return 0

    lax.fori_loop(0, 6, prepare, 0)

    lane1 = iota((1, 128), 1)
    placed = jnp.where(lane1 < 32, code, 0)
    placed = placed + left(placed, -32)
    placed = placed + left(placed, -64) + (lane1 >> 5)
    pb[0] = jnp.where(iota((512, 128), 0) == placed, 1.0, 0.0).astype(bf16)
    later = left(code, 32)
    placed = jnp.where(lane1 < 64, (later & -16) + (lane1 >> 5) * 8 + ((later >> 2) & 3) * 2, 0)
    placed = placed + left(placed, -64) + (lane1 >> 6)
    pb[1] = jnp.where(iota((512, 128), 0) == placed, 1.0, 0.0).astype(bf16)
    row = iota((288, 256), 0)
    col = iota((288, 256), 1)
    kind = (row >= 96).astype(i32) + (row >= 192).astype(i32)
    row = row - 96 * kind
    k0, r = row & 15, col & 15
    inside = jnp.where(
        kind == 0, (r >= k0).astype(i32), jnp.where(kind == 1, (r < k0 + 12).astype(i32), (r < k0 - 4).astype(i32)))
    same = (row >> 4) == ((col >> 4) & 7)
    windows[0:288, :] = jnp.where(same, inside, 0).astype(f32).astype(bf16)
    same = iota((16, 256), 0) == ((iota((16, 256), 1) >> 4) & 7)
    windows[288:304, :] = jnp.where(same, 1.0, 0.0).astype(bf16)

    vb[:, 48:64, :] = jnp.zeros((6, 16, 384), bf16)
    vb[:, 112:128, :] = jnp.zeros((6, 16, 384), bf16)

    pltpu.make_async_copy(send_a.at[pl.ds(0, NT - 1)], recv_a.at[pl.ds(0, NT - 1)], ra).wait()
    zf[...] = recv_a[...].astype(f32).reshape(512, 128)

    sums = []
    for rr in range(3):
        z = jnp.concatenate([zf[pl.ds(4 * rr + bh, NT, stride=16), :] for bh in range(4)], axis=0).T
        z0[rr] = z
        hi, lo = split2(z * z)
        sums.append(dot(windows[...], jnp.concatenate([hi, lo], axis=0)))
    suffix, e1, e2 = (jnp.concatenate([x[96 * i:96 * i + 96] for x in sums], axis=0) for i in range(3))
    whole = jnp.concatenate([x[288:296] for x in sums], axis=0)
    b2 = whole + next_block(whole)
    b4 = b2 + left(b2, 1)
    b8 = b4 + left(b4, 2)
    b16 = b8 + left(b8, 4)
    middle = next_block(b16 + left(whole, 8))
    middle = jnp.concatenate(
        [jnp.broadcast_to(middle[8 * rr + k:8 * rr + k + 1], (16, 128)) for rr in range(3) for k in range(6)], axis=0)
    half = (iota((288, 128), 1) >> 5) & 1
    power = suffix + left(e1, 9) + (middle + jnp.where(half == 0, left(e2, 41), left(e2, -22)))
    v = lax.rsqrt(power / TAPS + EPS)
    for e, x in enumerate((v, next_block(v), left(v, 1))):
        for part, y in enumerate(split2(x)):
            for sc in range(18):
                at = 64 * part + 16 * e
                vb[sc // 3, at:at + 16, 128 * (sc % 3):128 * (sc % 3) + 128] = y[16 * sc:16 * sc + 16]

    def pair(rr):
        lane16 = iota((16, 128), 1)
        for s2 in range(2):
            s = rr * 2 + s2
            norm = dot(tsel[s], vb[s])
            total = None
            for c in range(3):
                sc = s * 3 + c
                z = z0[rr, 16 * (3 * s2 + c):16 * (3 * s2 + c) + 16, :]
                z1 = next_block(z).astype(bf16)
                z = z.astype(bf16)
                lagged = jnp.concatenate([left(x, u) for u in range(11) for x in (z, z1)], axis=0)
                numer = dot(wt[sc, :, 0:352], lagged)
                scaled = norm[:, 128 * c:128 * c + 128].reshape(16, 16, 128) * invw[sc][:, None, :]
                term = numer.reshape(16, 16, 128) * scaled
                total = term if total is None else total + term
            ssc[s] = total.reshape(256, 128)
            coarse = pk[16 * s:16 * s + 16, :] >> 16
            for chunk in range(4):
                merged = None
                for low in range(4):
                    x = ssc[s, pl.ds(4 * chunk + low, 16, stride=16), :].astype(bf16)
                    for bit in range(4):
                        x = jnp.where((coarse & (1 << bit)) != 0, left(x, 1 << bit), x)
                    x = left(x, -8 * low)
                    merged = x if merged is None else jnp.where(((lane16 >> 3) & 3) == low, x, merged)
                aligned[chunk, 16 * s:16 * s + 16, :] = merged

    def send(k, which, rows):
        corr = jnp.concatenate(rows, axis=0)
        send_b[k] = dot(pb[which], corr).astype(bf16).reshape(NT, 16, 128)

        for by in TMPL:
            peer = tmpl_peer(me_t, by)
            pltpu.make_async_remote_copy(
                src_ref=send_b.at[k, peer], dst_ref=recv_b.at[k, me_t], send_sem=sb.at[k], recv_sem=rb.at[k],
                device_id={"tmpl": peer}, device_id_type=MESH).start()
        recv_b[k, me_t] = send_b[k, me_t]

    pair(0)
    send(0, 0, [aligned[c, 0:32, :] for c in range(4)])
    pair(1)
    pair(2)
    for k in range(2):
        send(1 + k, 1, [aligned[c, 32:96, :] for c in (2 * k, 2 * k + 1)])

    for k in range(2):
        marks = zf[pl.ds(12 + k, NT, stride=16), :]
        for u in range(4):
            mark = jnp.sum(marks[8 * u:8 * u + 8], axis=0, keepdims=True).astype(i32)
            chunk = lane1 & (1 if k else 3)
            key[4 * k + u:4 * k + u + 1, :] = jnp.where(mark > 0, chunk * 256 + mark - 1, -1)

    def onehot(n, _):
        line = iota((64, 128), 0)
        code = (line >> 4) * 256 + (line & 15) + n * 16
        found = None
        rows = pl.ds(pl.multiple_of(n * 32, 32), 32)
        for u in range(4):
            at = slice(128 * u, 128 * u + 128)
            hit = jnp.where(code == key[u:u + 1, :], 1.0, 0.0)
            ob[0, rows, at] = hit[:32].astype(bf16)
            ob[1, rows, at] = hit[32:].astype(bf16)
            found = hit[:16] if found is None else found + hit[:16]
            hit = jnp.where(code[:32] == key[4 + u:5 + u, :], 1.0, 0.0)
            ob[2, rows, at] = hit.astype(bf16)
            found = found + hit[:16]
        number = jnp.broadcast_to(jnp.sum(found, axis=1, keepdims=True), (16, 128)).astype(i32)
        parts = jnp.where(iota((16, 128), 1) < 64, number & 127, number >> 7)
        send_k[n] = parts.astype(f32).astype(bf16)
        return 0

    lax.fori_loop(0, NS, onehot, 0)

    for by in STN:
        peer = stn_peer(me_n, by)
        pltpu.make_async_remote_copy(
            src_ref=send_k.at[peer], dst_ref=recv_k.at[me_n], send_sem=sk, recv_sem=rk,
            device_id={"stn": peer}, device_id_type=MESH).start()
    recv_k[me_n] = send_k[me_n]

    k = iota((512, 512), 1)
    place = ((k >> 2) & 3) * 128 + (k >> 8) * 64 + ((k >> 4) & 1) * 32 + (k & 3) * 8 + ((k >> 5) & 7)
    q[...] = jnp.where(iota((512, 512), 0) == place, 1.0, 0.0).astype(bf16)

    def arrived(k):
        pltpu.make_async_copy(send_b.at[k, pl.ds(0, NT - 1)], recv_b.at[k, pl.ds(0, NT - 1)], rb.at[k]).wait()
        return recv_b[k].reshape(512, 128)

    stations = arrived(0)
    for h in range(2):
        acc[h] = dot(ob[h], stations)
    for h in range(2):
        stations = arrived(1 + h)
        for i in range(2):
            y = ((me_n >> 3) + 1 + i) & 1
            rows = pl.ds(pl.multiple_of(y * 256, 256), 256)
            part = acc[h, rows, :] + dot(ob[2, rows, :], stations)
            send_c[h, pl.ds(y * 8, 8)] = part.astype(bf16).reshape(8, 32, 128)

            for by in STN:
                if by[0] == 1 - i:
                    peer = stn_peer(me_n, by)
                    pltpu.make_async_remote_copy(
                        src_ref=send_c.at[h, peer], dst_ref=recv_c.at[h, me_n], send_sem=sc_.at[h],
                        recv_sem=rc.at[h], device_id={"stn": peer}, device_id_type=MESH).start()
        recv_c[h, me_n] = send_c[h, me_n]

    pltpu.make_async_copy(send_k.at[pl.ds(0, NS - 1)], recv_k.at[pl.ds(0, NS - 1)], rk).wait()
    found = jnp.sum(recv_k[...].astype(f32), axis=0)
    found = jnp.where(iota((16, 128), 1) < 64, found, found * 128.0)
    found = found + left(found, 64)
    scale = jnp.sqrt(f32(TAPS)) * lax.rsqrt(jnp.maximum(found, 1.0))

    moved = None
    for h in range(2):
        pltpu.make_async_copy(send_c.at[h, pl.ds(0, NS - 1)], recv_c.at[h, pl.ds(0, NS - 1)], rc.at[h]).wait()
        y = jnp.sum(recv_c[h].astype(f32), axis=0)
        y = jnp.concatenate([y[:16] * scale, y[16:] * scale], axis=1)
        hi, rest = y.astype(bf16), y - y.astype(bf16).astype(f32)
        mid, low = split2(rest)
        three = dot(jnp.concatenate([hi, mid, low], axis=0), q[256 * h:256 * h + 256, :])
        three = three[0:16] + three[16:32] + three[32:48]
        moved = three if moved is None else moved + three
    out[0] = moved[:, :256]
    out[1] = moved[:, 256:]

    pltpu.make_async_copy(send_a.at[pl.ds(0, NT - 1)], recv_a.at[pl.ds(0, NT - 1)], sa).wait()
    for rr in range(3):
        pltpu.make_async_copy(send_b.at[rr, pl.ds(0, NT - 1)], recv_b.at[rr, pl.ds(0, NT - 1)], sb.at[rr]).wait()
    pltpu.make_async_copy(send_k.at[pl.ds(0, NS - 1)], recv_k.at[pl.ds(0, NS - 1)], sk).wait()
    for h in range(2):
        pltpu.make_async_copy(send_c.at[h, pl.ds(0, NS - 1)], recv_c.at[h, pl.ds(0, NS - 1)], sc_.at[h]).wait()


def body(data, waves, slot_group, slot_local, moveout, chan_mask):
    vmem = pl.BlockSpec(memory_space=pltpu.VMEM)
    hbm = pl.BlockSpec(memory_space=pltpu.HBM)
    dma = pltpu.SemaphoreType.DMA
    return pl.pallas_call(
        kernel,
        out_shape=pltpu.VMEM((2, 16, 256), f32),
        in_specs=[hbm] * 6,
        out_specs=vmem,
        scratch_shapes=[
            pltpu.VMEM((24, 2, 32), bf16),
            pltpu.VMEM((18, 16, TAPS), bf16),
            pltpu.VMEM((6, 1, 16), i32),
            pltpu.VMEM((6, 16), i32),
            pltpu.VMEM((6, 16), i32),
            pltpu.SMEM((3, 6), i32),
            pltpu.VMEM((96, 128), i32),
            pltpu.VMEM((8, 128), i32),
            pltpu.VMEM((NT, 16, 128), bf16),
            pltpu.VMEM((NT, 16, 128), bf16),
            pltpu.VMEM((18, 256, 384), bf16),
            pltpu.VMEM((18, 16, 128), f32),
            pltpu.VMEM((6, 256, 128), bf16),
            pltpu.VMEM((2, 512, 128), bf16),
            pltpu.VMEM((304, 256), bf16),
            pltpu.VMEM((3, 128, 128), f32),
            pltpu.VMEM((512, 128), f32),
            pltpu.VMEM((6, 256, 128), f32),
            pltpu.VMEM((4, 96, 128), bf16),
            pltpu.VMEM((6, 128, 384), bf16),
            pltpu.VMEM((3, NT, 16, 128), bf16),
            pltpu.VMEM((3, NT, 16, 128), bf16),
            pltpu.VMEM((16, 128), i32),
            pltpu.VMEM((3, 512, 512), bf16),
            pltpu.VMEM((2, 512, 128), f32),
            pltpu.VMEM((2, NS, 32, 128), bf16),
            pltpu.VMEM((2, NS, 32, 128), bf16),
            pltpu.VMEM((NS, 16, 128), bf16),
            pltpu.VMEM((NS, 16, 128), bf16),
            pltpu.VMEM((512, 512), bf16),
            dma((5,)), dma, dma, dma, dma((3,)), dma((3,)), dma((2,)), dma((2,)), dma, dma,
        ],
        compiler_params=pltpu.CompilerParams(
            collective_id=0, has_side_effects=True, vmem_limit_bytes=60 * 2**20),
    )(
        jnp.transpose(data, (1, 2, 0, 3)).reshape(18, 2, 32),
        jnp.transpose(waves, (0, 2, 1, 3)).reshape(18, 16, TAPS),
        jnp.transpose(slot_group, (0, 2, 1)),
        slot_local, moveout, jnp.transpose(chan_mask),
    )


def solution(mesh):
    in_specs = (
        P(None, "stn", None, "tmpl"),
        P("stn", "tmpl", None, None),
        P("stn", "tmpl", None),
        P("stn", "tmpl"),
        P("stn", "tmpl"),
        P("stn", None),
    )
    out_specs = P(None, ("tmpl", "stn"), None)
    return jax.shard_map(body, mesh=mesh, in_specs=in_specs, out_specs=out_specs, check_vma=False)
```

```python
import functools

import jax
import jax.numpy as jnp
from jax import lax
from jax.experimental import pallas as pl
from jax.experimental.pallas import tpu as pltpu
from jax.sharding import PartitionSpec as P

NT = 32
NS = 16
TAPS = 300
EPS = 1e-06
MESH = pl.DeviceIdType.MESH
f32, bf16, i32 = jnp.float32, jnp.bfloat16, jnp.int32


def iota(shape, axis):
    return lax.broadcasted_iota(i32, shape, axis)


def left(x, by):
    by %= 128
    return x if by == 0 else pltpu.roll(x, 128 - by, axis=x.ndim - 1)


def next_block(x):
    half = (iota(x.shape, x.ndim - 1) >> 5) & 1
    return jnp.where(half == 0, left(x, 32), left(x, -31))


def split2(x):
    hi = x.astype(bf16)
    return hi, (x - hi.astype(f32)).astype(bf16)


def dot(a, b):
    return jnp.dot(a, b, preferred_element_type=f32)


def around(step, size):
    return min(step, size - step)


TMPL = sorted(
    ((x, y, c) for x in range(4) for y in range(4) for c in range(2) if x or y or c),
    key=lambda d: -(around(d[0], 4) + 2 * around(d[1], 4) + 0.5 * d[2]))
STN = sorted(
    ((y, z) for y in range(2) for z in range(8) if y or z), key=lambda d: -(d[0] + around(d[1], 8)))


def tmpl_peer(me, by):
    x, y, c = by
    return ((((me >> 3) + x) & 3) << 3) | ((((me >> 1) + y) & 3) << 1) | ((me + c) & 1)


def stn_peer(me, by):
    y, z = by
    return ((((me >> 3) + y) & 1) << 3) | ((me + z) & 7)


def kernel(
    data_in, waves_in, group_in, local_in, move_in, mask_in, out,
    data_v, w0, group_v, local_v, move_v, cm, pk, codes,
    send_a, recv_a, wt, invw, tsel, pb, windows, z0, zf, ssc, aligned, vb,
    send_b, recv_b, key, ob, acc, send_c, recv_c, send_k, recv_k, q,
    si, sw, sa, ra, sb, rb, sc_, rc, sk, rk,
):
    me_t, me_n = lax.axis_index("tmpl"), lax.axis_index("stn")
    small = [
        pltpu.make_async_copy(data_in, data_v.at[pl.ds(0, 18)], si.at[0]),
        pltpu.make_async_copy(group_in, group_v, si.at[1]),
        pltpu.make_async_copy(local_in, local_v, si.at[2]),
        pltpu.make_async_copy(move_in, move_v, si.at[3]),
        pltpu.make_async_copy(mask_in, cm, si.at[4]),
    ]
    large = pltpu.make_async_copy(waves_in, w0, sw)
    for copy in small:
        copy.start()
    large.start()

    bar = pltpu.get_barrier_semaphore()

    for by in sorted(TMPL + STN, key=lambda d: -(
            around(d[0], 4) + 2 * around(d[1], 4) if len(d) == 3 else d[0] + around(d[1], 8))):
        to = {"tmpl": tmpl_peer(me_t, by)} if len(by) == 3 else {"stn": stn_peer(me_n, by)}
        pl.semaphore_signal(bar, inc=1, device_id=to, device_id_type=MESH)
    for copy in small:
        copy.wait()

    sub16, lane16s = iota((16, 16), 0), iota((16, 16), 1)
    codes[...] = jnp.zeros((8, 128), i32)
    for s in range(6):
        group = jnp.broadcast_to(group_v[s], (16, 16))
        column = jnp.sum(jnp.where(sub16 == lane16s, group, 0).astype(f32), axis=1, keepdims=True).astype(i32)
        same = group == column
        rank_rows = jnp.sum(jnp.where(same & (lane16s < sub16), 1.0, 0.0), axis=1, keepdims=True)
        rank_lanes = jnp.sum(jnp.where(same & (sub16 < lane16s), 1.0, 0.0), axis=0, keepdims=True)
        fields = (move_v[s:s + 1, :] << 11) | ((local_v[s:s + 1, :] + 1) << 2) | ((s & 1) * 2)
        fields = jnp.where(sub16 == lane16s, jnp.broadcast_to(fields, (16, 16)), 0)
        fields = jnp.sum(fields.astype(f32), axis=1, keepdims=True) + rank_rows
        pk[16 * s:16 * s + 16, :] = jnp.broadcast_to(fields, (16, 128)).astype(i32)
        codes[s:s + 1, 0:16] = group_v[s] * 16 + ((s & 1) * 2 + rank_lanes.astype(i32)) * 4
    spread = pltpu.roll(codes[...].astype(f32), 0, axis=1, stride=16, stride_axis=0)
    code = jnp.sum(spread, axis=0, keepdims=True).astype(i32)

    parts = []
    row24, lane24 = iota((24, 128), 0), iota((24, 128), 1)
    third = (row24 >= 6).astype(i32) + (row24 >= 12).astype(i32)
    keep = ((lane24 >> 4) == row24 - 6 * third) & (row24 < 18)
    for b in range(2):
        samples = data_v[:, b, :]
        for half in range(2):
            widen = iota((32, 128), 0) == half * 16 + (iota((32, 128), 1) & 15)
            parts.append(jnp.where(keep, dot(samples, jnp.where(widen, 1.0, 0.0).astype(bf16)), 0.0))
    source = iota((16, 128), 1)
    dest = iota((16, 128), 0)
    bh = (source >= 24).astype(i32) + (source >= 48).astype(i32) + (source >= 72).astype(i32)
    sc24 = source - 24 * bh
    gather = dest == ((sc24 >= 6).astype(i32) + (sc24 >= 12).astype(i32)) * 4 + bh
    gather = jnp.where(gather & (sc24 < 18) & (source < 96), 1.0, 0.0).astype(bf16)
    stacked = jnp.concatenate(parts + [jnp.zeros((32, 128), f32)], axis=0).astype(bf16)
    dtile = dot(gather, stacked)
    lane = iota((96, 128), 1)
    packed = pk[...]
    mine = (lane >> 4) == (me_t & 7)
    pair_of = iota((96, 128), 0) >> 5
    spot = jnp.where(pair_of == 0, (lane & 15) >> 2, ((lane & 15) >> 1) + 4 - 4 * pair_of)
    id_rows = jnp.where(mine & (spot == (packed & 3)), (packed >> 2) & 511, 0)
    first = (code & -16) + 12 + (iota((1, 128), 1) >= 32).astype(i32)
    pick = iota((512, 96), 0) == first[:, 0:96]
    ids = dot(jnp.where(pick, 1.0, 0.0).astype(bf16), id_rows.astype(f32).astype(bf16))
    send_a[...] = (ids.reshape(NT, 16, 128) + dtile[None]).astype(bf16)
    recv_a[me_t] = send_a[me_t]

    pl.semaphore_wait(bar, NT - 1 + NS - 1)

    for by in TMPL:
        peer = tmpl_peer(me_t, by)
        pltpu.make_async_remote_copy(
            src_ref=send_a.at[peer], dst_ref=recv_a.at[me_t], send_sem=sa, recv_sem=ra,
            device_id={"tmpl": peer}, device_id_type=MESH).start()

    large.wait()

    def prepare(s, _):
        rows = pk[pl.ds(pl.multiple_of(s * 16, 16), 16), :]
        fine = (rows >> 11) & 31
        lane16 = iota((16, 128), 1)
        usable = [cm[c, s].astype(f32) for c in range(3)]
        total = usable[0] + usable[1] + usable[2]
        per = jnp.where(total > 2.5, 1.0 / 3.0, jnp.where(total > 1.5, 0.5, 1.0)) / TAPS
        for c in range(3):
            sc = s * 3 + c
            x = [w0[sc, :, 0:128].astype(f32), w0[sc, :, 128:256].astype(f32),
                 jnp.pad(w0[sc, :, 256:TAPS].astype(f32), ((0, 0), (0, 384 - TAPS)))]
            power = jnp.sum(x[0] * x[0] + x[1] * x[1] + x[2] * x[2], axis=1, keepdims=True)
            invw[sc] = jnp.broadcast_to(lax.rsqrt(power / TAPS + EPS), (16, 128)) * (usable[c] * per)
            for bit in range(5):
                by = 1 << bit
                y = [pltpu.roll(v, by, axis=1) for v in x]
                wide = [jnp.where(lane16 >= by, y[j], y[j - 1] if j else 0.0) for j in range(3)]
                on = (fine & by) != 0
                x = [jnp.where(on, wide[j], x[j]) for j in range(3)]
            k0 = iota((16, 16, 128), 1)
            l3 = iota((16, 16, 128), 2)
            y = [
                pltpu.roll(jnp.broadcast_to(v[:, None, :], (16, 16, 128)), 0, axis=2, stride=1, stride_axis=1)
                for v in x
            ]
            for j in range(3):
                t = jnp.where(l3 >= k0, y[j], y[j - 1] if j else 0.0)
                wt[sc, :, 128 * j:128 * j + 128] = t.reshape(256, 128).astype(bf16)
        k0 = iota((16, 16, 128), 1)
        l3 = iota((16, 16, 128), 2)
        hit = (l3 & 63) == k0 + fine[:, None, :]
        tsel[s] = jnp.where(hit, 1.0, 0.0).reshape(256, 128).astype(bf16)
        return 0

    lax.fori_loop(0, 6, prepare, 0)

    lane1 = iota((1, 128), 1)
    placed = jnp.where(lane1 < 32, code, 0)
    placed = placed + left(placed, -32)
    placed = placed + left(placed, -64) + (lane1 >> 5)
    pb[0] = jnp.where(iota((512, 128), 0) == placed, 1.0, 0.0).astype(bf16)
    later = left(code, 32)
    placed = jnp.where(lane1 < 64, (later & -16) + (lane1 >> 5) * 8 + ((later >> 2) & 3) * 2, 0)
    placed = placed + left(placed, -64) + (lane1 >> 6)
    pb[1] = jnp.where(iota((512, 128), 0) == placed, 1.0, 0.0).astype(bf16)
    row = iota((288, 256), 0)
    col = iota((288, 256), 1)
    kind = (row >= 96).astype(i32) + (row >= 192).astype(i32)
    row = row - 96 * kind
    k0, r = row & 15, col & 15
    inside = jnp.where(
        kind == 0, (r >= k0).astype(i32), jnp.where(kind == 1, (r < k0 + 12).astype(i32), (r < k0 - 4).astype(i32)))
    same = (row >> 4) == ((col >> 4) & 7)
    windows[0:288, :] = jnp.where(same, inside, 0).astype(f32).astype(bf16)
    same = iota((16, 256), 0) == ((iota((16, 256), 1) >> 4) & 7)
    windows[288:304, :] = jnp.where(same, 1.0, 0.0).astype(bf16)

    vb[:, 48:64, :] = jnp.zeros((6, 16, 384), bf16)
    vb[:, 112:128, :] = jnp.zeros((6, 16, 384), bf16)

    pltpu.make_async_copy(send_a.at[pl.ds(0, NT - 1)], recv_a.at[pl.ds(0, NT - 1)], ra).wait()
    zf[...] = recv_a[...].astype(f32).reshape(512, 128)

    sums = []
    for rr in range(3):
        z = jnp.concatenate([zf[pl.ds(4 * rr + bh, NT, stride=16), :] for bh in range(4)], axis=0).T
        z0[rr] = z
        hi, lo = split2(z * z)
        sums.append(dot(windows[...], jnp.concatenate([hi, lo], axis=0)))
    suffix, e1, e2 = (jnp.concatenate([x[96 * i:96 * i + 96] for x in sums], axis=0) for i in range(3))
    whole = jnp.concatenate([x[288:296] for x in sums], axis=0)
    b2 = whole + next_block(whole)
    b4 = b2 + left(b2, 1)
    b8 = b4 + left(b4, 2)
    b16 = b8 + left(b8, 4)
    middle = next_block(b16 + left(whole, 8))
    middle = jnp.concatenate(
        [jnp.broadcast_to(middle[8 * rr + k:8 * rr + k + 1], (16, 128)) for rr in range(3) for k in range(6)], axis=0)
    half = (iota((288, 128), 1) >> 5) & 1
    power = suffix + left(e1, 9) + (middle + jnp.where(half == 0, left(e2, 41), left(e2, -22)))
    v = lax.rsqrt(power / TAPS + EPS)
    for e, x in enumerate((v, next_block(v), left(v, 1))):
        for part, y in enumerate(split2(x)):
            for sc in range(18):
                at = 64 * part + 16 * e
                vb[sc // 3, at:at + 16, 128 * (sc % 3):128 * (sc % 3) + 128] = y[16 * sc:16 * sc + 16]

    def pair(rr):
        lane16 = iota((16, 128), 1)
        for s2 in range(2):
            s = rr * 2 + s2
            norm = dot(tsel[s], vb[s])
            total = None
            for c in range(3):
                sc = s * 3 + c
                z = z0[rr, 16 * (3 * s2 + c):16 * (3 * s2 + c) + 16, :]
                z1 = next_block(z).astype(bf16)
                z = z.astype(bf16)
                lagged = jnp.concatenate([left(x, u) for u in range(11) for x in (z, z1)], axis=0)
                numer = dot(wt[sc, :, 0:352], lagged)
                scaled = norm[:, 128 * c:128 * c + 128].reshape(16, 16, 128) * invw[sc][:, None, :]
                term = numer.reshape(16, 16, 128) * scaled
                total = term if total is None else total + term
            ssc[s] = total.reshape(256, 128)
            coarse = pk[16 * s:16 * s + 16, :] >> 16
            for chunk in range(4):
                merged = None
                for low in range(4):
                    x = ssc[s, pl.ds(4 * chunk + low, 16, stride=16), :].astype(bf16)
                    for bit in range(4):
                        x = jnp.where((coarse & (1 << bit)) != 0, left(x, 1 << bit), x)
                    x = left(x, -8 * low)
                    merged = x if merged is None else jnp.where(((lane16 >> 3) & 3) == low, x, merged)
                aligned[chunk, 16 * s:16 * s + 16, :] = merged

    def send(k, which, rows):
        corr = jnp.concatenate(rows, axis=0)
        send_b[k] = dot(pb[which], corr).astype(bf16).reshape(NT, 16, 128)

        for by in TMPL:
            peer = tmpl_peer(me_t, by)
            pltpu.make_async_remote_copy(
                src_ref=send_b.at[k, peer], dst_ref=recv_b.at[k, me_t], send_sem=sb.at[k], recv_sem=rb.at[k],
                device_id={"tmpl": peer}, device_id_type=MESH).start()
        recv_b[k, me_t] = send_b[k, me_t]

    pair(0)
    send(0, 0, [aligned[c, 0:32, :] for c in range(4)])
    pair(1)
    pair(2)
    for k in range(2):
        send(1 + k, 1, [aligned[c, 32:96, :] for c in (2 * k, 2 * k + 1)])

    for k in range(2):
        marks = zf[pl.ds(12 + k, NT, stride=16), :]
        for u in range(4):
            mark = jnp.sum(marks[8 * u:8 * u + 8], axis=0, keepdims=True).astype(i32)
            chunk = lane1 & (1 if k else 3)
            key[4 * k + u:4 * k + u + 1, :] = jnp.where(mark > 0, chunk * 256 + mark - 1, -1)

    def onehot(n, _):
        line = iota((64, 128), 0)
        code = (line >> 4) * 256 + (line & 15) + n * 16
        found = None
        rows = pl.ds(pl.multiple_of(n * 32, 32), 32)
        for u in range(4):
            at = slice(128 * u, 128 * u + 128)
            hit = jnp.where(code == key[u:u + 1, :], 1.0, 0.0)
            ob[0, rows, at] = hit[:32].astype(bf16)
            ob[1, rows, at] = hit[32:].astype(bf16)
            found = hit[:16] if found is None else found + hit[:16]
            hit = jnp.where(code[:32] == key[4 + u:5 + u, :], 1.0, 0.0)
            ob[2, rows, at] = hit.astype(bf16)
            found = found + hit[:16]
        number = jnp.sum(found, axis=1, keepdims=True)
        along = jnp.where(iota((16, 128), 0) == iota((16, 128), 1), number, 0.0)
        send_k[n, 0:1, :] = jnp.sum(along, axis=0, keepdims=True)
        return 0

    lax.fori_loop(0, NS, onehot, 0)

    for by in STN:
        peer = stn_peer(me_n, by)
        pltpu.make_async_remote_copy(
            src_ref=send_k.at[peer, pl.ds(0, 1)], dst_ref=recv_k.at[me_n, pl.ds(0, 1)], send_sem=sk, recv_sem=rk,
            device_id={"stn": peer}, device_id_type=MESH).start()
    recv_k[me_n, 0:1, :] = send_k[me_n, 0:1, :]

    k = iota((512, 512), 1)
    place = ((k >> 2) & 3) * 128 + (k >> 8) * 64 + ((k >> 4) & 1) * 32 + (k & 3) * 8 + ((k >> 5) & 7)
    q[...] = jnp.where(iota((512, 512), 0) == place, 1.0, 0.0).astype(bf16)

    def arrived(k):
        pltpu.make_async_copy(send_b.at[k, pl.ds(0, NT - 1)], recv_b.at[k, pl.ds(0, NT - 1)], rb.at[k]).wait()
        return recv_b[k].reshape(512, 128)

    stations = arrived(0)
    for h in range(2):
        acc[h] = dot(ob[h], stations)
    for h in range(2):
        stations = arrived(1 + h)
        for i in range(2):
            y = ((me_n >> 3) + 1 + i) & 1
            rows = pl.ds(pl.multiple_of(y * 256, 256), 256)
            part = acc[h, rows, :] + dot(ob[2, rows, :], stations)
            send_c[h, pl.ds(y * 8, 8)] = part.astype(bf16).reshape(8, 32, 128)

            for by in STN:
                if by[0] == 1 - i:
                    peer = stn_peer(me_n, by)
                    pltpu.make_async_remote_copy(
                        src_ref=send_c.at[h, peer], dst_ref=recv_c.at[h, me_n], send_sem=sc_.at[h],
                        recv_sem=rc.at[h], device_id={"stn": peer}, device_id_type=MESH).start()
        recv_c[h, me_n] = send_c[h, me_n]

    pltpu.make_async_copy(send_k.at[pl.ds(0, NS - 1), pl.ds(0, 1)], recv_k.at[pl.ds(0, NS - 1), pl.ds(0, 1)], rk).wait()
    found = jnp.broadcast_to(jnp.sum(recv_k[:, 0:1, :], axis=0), (16, 128))
    found = jnp.where(iota((16, 128), 0) == iota((16, 128), 1), found, 0.0)
    found = jnp.broadcast_to(jnp.sum(found, axis=1, keepdims=True), (16, 128))
    scale = jnp.sqrt(f32(TAPS)) * lax.rsqrt(jnp.maximum(found, 1.0))

    moved = None
    for h in range(2):
        pltpu.make_async_copy(send_c.at[h, pl.ds(0, NS - 1)], recv_c.at[h, pl.ds(0, NS - 1)], rc.at[h]).wait()
        y = jnp.sum(recv_c[h].astype(f32), axis=0)
        y = jnp.concatenate([y[:16] * scale, y[16:] * scale], axis=1)
        hi, rest = y.astype(bf16), y - y.astype(bf16).astype(f32)
        mid, low = split2(rest)
        three = dot(jnp.concatenate([hi, mid, low], axis=0), q[256 * h:256 * h + 256, :])
        three = three[0:16] + three[16:32] + three[32:48]
        moved = three if moved is None else moved + three
    out[0] = moved[:, :256]
    out[1] = moved[:, 256:]

    pltpu.make_async_copy(send_a.at[pl.ds(0, NT - 1)], recv_a.at[pl.ds(0, NT - 1)], sa).wait()
    for rr in range(3):
        pltpu.make_async_copy(send_b.at[rr, pl.ds(0, NT - 1)], recv_b.at[rr, pl.ds(0, NT - 1)], sb.at[rr]).wait()
    pltpu.make_async_copy(send_k.at[pl.ds(0, NS - 1), pl.ds(0, 1)], recv_k.at[pl.ds(0, NS - 1), pl.ds(0, 1)], sk).wait()
    for h in range(2):
        pltpu.make_async_copy(send_c.at[h, pl.ds(0, NS - 1)], recv_c.at[h, pl.ds(0, NS - 1)], sc_.at[h]).wait()


def body(data, waves, slot_group, slot_local, moveout, chan_mask):
    vmem = pl.BlockSpec(memory_space=pltpu.VMEM)
    hbm = pl.BlockSpec(memory_space=pltpu.HBM)
    dma = pltpu.SemaphoreType.DMA
    return pl.pallas_call(
        kernel,
        out_shape=pltpu.VMEM((2, 16, 256), f32),
        in_specs=[hbm] * 6,
        out_specs=vmem,
        scratch_shapes=[
            pltpu.VMEM((24, 2, 32), bf16),
            pltpu.VMEM((18, 16, TAPS), bf16),
            pltpu.VMEM((6, 1, 16), i32),
            pltpu.VMEM((6, 16), i32),
            pltpu.VMEM((6, 16), i32),
            pltpu.SMEM((3, 6), i32),
            pltpu.VMEM((96, 128), i32),
            pltpu.VMEM((8, 128), i32),
            pltpu.VMEM((NT, 16, 128), bf16),
            pltpu.VMEM((NT, 16, 128), bf16),
            pltpu.VMEM((18, 256, 384), bf16),
            pltpu.VMEM((18, 16, 128), f32),
            pltpu.VMEM((6, 256, 128), bf16),
            pltpu.VMEM((2, 512, 128), bf16),
            pltpu.VMEM((304, 256), bf16),
            pltpu.VMEM((3, 128, 128), f32),
            pltpu.VMEM((512, 128), f32),
            pltpu.VMEM((6, 256, 128), f32),
            pltpu.VMEM((4, 96, 128), bf16),
            pltpu.VMEM((6, 128, 384), bf16),
            pltpu.VMEM((3, NT, 16, 128), bf16),
            pltpu.VMEM((3, NT, 16, 128), bf16),
            pltpu.VMEM((16, 128), i32),
            pltpu.VMEM((3, 512, 512), bf16),
            pltpu.VMEM((2, 512, 128), f32),
            pltpu.VMEM((2, NS, 32, 128), bf16),
            pltpu.VMEM((2, NS, 32, 128), bf16),
            pltpu.VMEM((NS, 8, 128), f32),
            pltpu.VMEM((NS, 8, 128), f32),
            pltpu.VMEM((512, 512), bf16),
            dma((5,)), dma, dma, dma, dma((3,)), dma((3,)), dma((2,)), dma((2,)), dma, dma,
        ],
        compiler_params=pltpu.CompilerParams(
            collective_id=0, has_side_effects=True, vmem_limit_bytes=60 * 2**20),
    )(
        jnp.transpose(data, (1, 2, 0, 3)).reshape(18, 2, 32),
        jnp.transpose(waves, (0, 2, 1, 3)).reshape(18, 16, TAPS),
        jnp.transpose(slot_group, (0, 2, 1)),
        slot_local, moveout, jnp.transpose(chan_mask),
    )


def solution(mesh):
    in_specs = (
        P(None, "stn", None, "tmpl"),
        P("stn", "tmpl", None, None),
        P("stn", "tmpl", None),
        P("stn", "tmpl"),
        P("stn", "tmpl"),
        P("stn", None),
    )
    out_specs = P(None, ("tmpl", "stn"), None)
    return jax.shard_map(body, mesh=mesh, in_specs=in_specs, out_specs=out_specs, check_vma=False)
```
